128 devices in a mesh: expert: 8 (over z, core), dp: 16 (over y, x).
Axes of the slice: x: 4, y: 4, z: 4, core: 2. Of those that a mesh axis runs over, the one named last changes fastest.
Arguments:
- hidden_in: bfloat16 [2, 9216, 768], P(None, ('expert', 'dp')), may hold values from -6 to 6
- lengths: int32 [2, 8, 3], P(None, 'expert'), may hold values from 1 to 1116, as said below
- routes: int32 [2, 9216, 2], P(None, ('expert', 'dp')), may hold values from 0 to 7, all different within a row; in each aligned block of 72 rows (0 to 71, 72 to 143, ..., all dimensions but the last counted through in order) at most 20 rows name the same one
- norm_gains: bfloat16 [4, 768], P(None, ('expert', 'dp')), may hold values from 0.5 to 1.5
- qkv_weights: bfloat16 [2, 3, 768, 768], P(None, None, ('expert', 'dp')), may hold values from -0.21875 to 0.21875
- out_weights: bfloat16 [2, 768, 768], P(None, ('expert', 'dp')), may hold values from -0.4375 to 0.4375
- rel_table: bfloat16 [384], P(('expert', 'dp')), may hold values from -3 to 3
- ffn_in: bfloat16 [768, 3072], P(('expert', 'dp')), may hold values from -0.21875 to 0.21875
- ffn_out: bfloat16 [3072, 768], P(('expert', 'dp')), may hold values from -0.109375 to 0.109375
- router: bfloat16 [768, 8], P(('expert', 'dp')), may hold values from -0.15625 to 0.15625
- expert_in: bfloat16 [8, 768, 3072], P('expert', 'dp'), may hold values from -0.21875 to 0.21875
- expert_out: bfloat16 [8, 3072, 768], P('expert', 'dp'), may hold values from -0.109375 to 0.109375
- cotangent: bfloat16 [2, 9216, 768], P(None, ('expert', 'dp')), may hold values from -6 to 6
Outputs:
- hidden_out: float32 [2, 9216, 768], P(None, ('expert', 'dp'))
- grad_input: float32 [2, 9216, 768], P(None, ('expert', 'dp'))
- grad_gains: float32 [4, 768], P(None, ('expert', 'dp'))
- grad_qkv: float32 [2, 3, 768, 768], P(None, None, ('expert', 'dp'))
- grad_out_weights: float32 [2, 768, 768], P(None, ('expert', 'dp'))
- grad_rel_table: float32 [384], P(('expert', 'dp'))
- grad_ffn_in: float32 [768, 3072], P(('expert', 'dp'))
- grad_ffn_out: float32 [3072, 768], P(('expert', 'dp'))
- grad_router: float32 [768, 8], P(('expert', 'dp'))
- grad_expert_in: float32 [8, 768, 3072], P('expert', 'dp')
- grad_expert_out: float32 [8, 3072, 768], P('expert', 'dp')
The draws below stay inside these ranges and needn't reach their ends.
Inputs may be any that keep to these rules, and one draw needn't show every extreme that they name: In each micro-batch and group the 3 lengths add up to 1152; one of them, at a place drawn from the seed, is 1116 and reaches from the group's first device to its last. `routes`: each token names two different experts. Among the 72 tokens of one device in one micro-batch no expert is named more than 20 times; in some devices' tokens one expert is named exactly 20 times.
All inputs are finite; a program needn't handle non-finite values.
Results may differ from the reference program's by a relative error of at most 0.04.
Values may be sent and summed in bfloat16 or wider, within the bound.
No kernel may reach another device: no remote copies, remote signals or barrier semaphores. Data moves between devices by JAX's collectives and lax.ppermute only.
A program may use at most 256 MiB of HBM per device.

```python
import math
import jax
import jax.numpy as jnp
import numpy as np
from jax import lax

D = 768
HEADS = 12
HEAD_DIM = 64
FF = 3072
BUCKETS = 16
MICRO = 2
DOCS = 3
TOK_DEV = 72
EXPERTS = 8
CAP = 20
GROUP = 1152
LONG = 1116
TOKENS = 9216
N_EXPERT = 8
N_DP = 16


def draw_lengths(key, part):
    key = jax.random.fold_in(key, 11)
    first_key, place_key = jax.random.split(key)
    remainder = GROUP - LONG
    first_part = jax.random.randint(first_key, (MICRO, N_EXPERT), 1, remainder, dtype=jnp.int32)
    second_part = remainder - first_part
    long_place = jax.random.randint(place_key, (MICRO, N_EXPERT), 0, DOCS, dtype=jnp.int32)
    position = jnp.arange(DOCS, dtype=jnp.int32)[None, None, :]
    other_rank = position - (position > long_place[:, :, None]).astype(jnp.int32)
    shorter = jnp.where(other_rank == 0, first_part[:, :, None], second_part[:, :, None])
    return jnp.where(position == long_place[:, :, None], LONG, shorter).astype(jnp.int32)


def levels(key, shape, shards, smallest, top_value):
    factor_of, own = 1.0, jax.random.fold_in(key, 6)
    for dim, blocks in shards:
        steps = jnp.exp(jax.random.uniform(jax.random.fold_in(own, dim), (blocks,), jnp.float32, smallest / len(shards), top_value / len(shards)))
        factor_of = factor_of * jnp.repeat(steps, shape[dim] // blocks).reshape([-1 if axis == dim else 1 for axis in range(len(shape))])
    return factor_of


def assign_block(key, own, number, rows, number_of, top, limit, lean):
    order = jax.random.permutation(key, number_of)
    packed, ordinary = load_shares(number_of, rows * top, limit, lean, True), load_shares(number_of, rows * top, limit, lean, False)
    places = jnp.arange(number_of)

    def named(sizes, turn):
        used = int((sizes > 0).sum())
        fixed = max(1, used // 4)
        moved = fixed + (places - fixed + turn * (used - fixed)) % max(1, number_of - fixed)
        return jnp.zeros((number_of,), jnp.int32).at[order[jnp.where(places < fixed, places, moved)]].set(jnp.asarray(sizes, jnp.int32))

    sizes = jnp.where(number % 4 == 0, named(packed, number // 4), named(ordinary, number - number // 4 - 1))
    mixed = jax.random.permutation(jax.random.fold_in(own, 3), number_of)
    source_of, sink = mixed[0:number_of // 2 * 2:2], mixed[1:number_of // 2 * 2:2]
    margin = jnp.minimum(sizes[source_of] - 1, limit - sizes[sink]) // 2
    margin = jnp.where((source_of == order[0]) | (sink == order[0]) | (sizes[sink] == 0), 0, jnp.maximum(margin, 0))
    moved = jax.random.randint(jax.random.fold_in(own, 4), (number_of // 2,), 0, 1 << 20) % (margin + 1)
    sizes = sizes.at[source_of].add(-moved).at[sink].add(moved)
    members = jnp.searchsorted(jnp.cumsum(sizes), jnp.arange(rows * top), side="right").astype(jnp.int32)
    table = members.reshape(top, rows).T
    table = table[jax.random.permutation(jax.random.fold_in(own, 1), rows)]
    turn = jax.random.randint(jax.random.fold_in(own, 2), (rows, 1), 0, top)
    return jnp.take_along_axis(table, (jnp.arange(top)[None, :] + turn) % top, axis=1)


def load_shares(count, total, reach, slope, full):
    loads = [(1 << 20) // math.isqrt(grade ** slope) + 1 for grade in range(1, count + 1)]
    largest = reach if full else min(reach, max(-(-total // count), total * loads[0] // sum(loads)))
    least = 1 if total - largest >= count - 1 else 0
    given, spare = [largest] + [least] * (count - 1), total - largest - least * (count - 1)
    while spare > 0:
        candidates = [i for i in range(1, count) if given[i] < largest] or [i for i in range(1, count) if given[i] < reach]
        mass, budget = sum([loads[i] for i in candidates]), spare
        for i in candidates:
            addition = min(reach - given[i], max(1, budget * loads[i] // mass), spare)
            given[i] = given[i] + addition
            spare = spare - addition
    return np.array(given)


def centred(stream_key, dims, width, bound, cuts=(), held_as=jnp.bfloat16):
    gain = levels(stream_key, dims, cuts, -0.22, 0.18) if cuts else 1.0
    array = jax.random.normal(stream_key, dims, jnp.float32) * width * gain
    return jnp.minimum(jnp.maximum(array, -bound), bound).astype(held_as)


def setup_inputs(seed: int = 0) -> dict:
    arg_keys = jax.random.split(jax.random.key(seed), 14)
    hidden_in = centred(arg_keys[0], (MICRO, TOKENS, D), 1.0, 6.0, ((1, 128),))
    lengths = draw_lengths(jax.random.fold_in(arg_keys[13], 71), 0)
    routes_keys = jax.random.split(jax.random.fold_in(arg_keys[2], 1), MICRO * TOKENS // TOK_DEV)
    routes_turns = jax.random.permutation(jax.random.fold_in(arg_keys[2], 3), MICRO * TOKENS // TOK_DEV)
    routes = jax.vmap(lambda own, number: assign_block(jax.random.fold_in(arg_keys[2], 2), own, number, TOK_DEV, EXPERTS, 2, CAP, 1))(routes_keys, routes_turns).reshape((MICRO, TOKENS, 2))
    norm_gains = jnp.clip(1.0 + 0.1 * jax.random.normal(arg_keys[3], (4, D), jnp.float32), 0.5, 1.5).astype(jnp.bfloat16)
    qkv_weights = centred(arg_keys[4], (2, 3, D, D), D ** -0.5, 0.21875, ((2, 128),))
    out_weights = centred(arg_keys[5], (2, D, D), (D // 4) ** -0.5, 0.4375, ((1, 128),))
    rel_table = centred(arg_keys[6], (2 * HEADS * BUCKETS,), 0.5, 3.0, ((0, 128),))
    ffn_in = centred(arg_keys[7], (D, FF), D ** -0.5, 0.21875, ((0, 128),))
    ffn_out = centred(arg_keys[8], (FF, D), FF ** -0.5, 0.109375, ((0, 128),))
    router = centred(arg_keys[9], (D, EXPERTS), (2 * D) ** -0.5, 0.15625, ((0, 128),))
    expert_in = centred(arg_keys[10], (EXPERTS, D, FF), D ** -0.5, 0.21875, ((0, 8), (1, 16)))
    expert_out = centred(arg_keys[11], (EXPERTS, FF, D), FF ** -0.5, 0.109375, ((0, 8), (1, 16)))
    cotangent = centred(arg_keys[12], (MICRO, TOKENS, D), 1.0, 6.0, ((1, 128),))
    return {"hidden_in": hidden_in, "lengths": lengths, "routes": routes, "norm_gains": norm_gains, "qkv_weights": qkv_weights, "out_weights": out_weights, "rel_table": rel_table, "ffn_in": ffn_in, "ffn_out": ffn_out, "router": router, "expert_in": expert_in, "expert_out": expert_out, "cotangent": cotangent}


precise = lax.Precision.HIGHEST
EPSILON = 1e-06
NEGATIVE = -1e+30

@jax.custom_vjp
def low(v):
    return lax.optimization_barrier(v.astype(jnp.bfloat16)).astype(jnp.float32)

@jax.custom_vjp
def low_back(v):
    return v

def low_keep(v):
    return (low(v), None)

def low_pass(kept, grad):
    return (grad,)

def back_keep(v):
    return (v, None)

def back_low(kept, grad):
    return (low(grad),)
low.defvjp(low_keep, low_pass)
low_back.defvjp(back_keep, back_low)

def normalize(values, scales):
    return values * lax.rsqrt(lax.optimization_barrier(jnp.mean(values * values, axis=-1, keepdims=True)) + EPSILON) * scales

def bucket_index(distance):
    distance = jnp.maximum(distance, 0)
    result = jnp.minimum(distance, 7)
    for exponent in range(3, 11):
        result = result + (distance >= 2 ** exponent).astype(jnp.int32)
    return result

def document_of(bounds, position):
    doc_ends = jnp.cumsum(bounds)
    return lax.optimization_barrier(jnp.sum((position[:, None] >= doc_ends[None, :]).astype(jnp.int32), axis=1))

def attention_group(stream, scales, weights, w_out, bias_table, bounds):
    normed = low(normalize(stream, scales))
    queries = low_back(low(jnp.dot(normed, weights[0], precision=precise)))
    keys_all = low_back(low(jnp.dot(normed, weights[1], precision=precise)))
    values_all = low_back(low(jnp.dot(normed, weights[2], precision=precise)))
    position = jnp.arange(GROUP, dtype=jnp.int32)
    documents = document_of(bounds, position)
    allowed = (position[None, :] <= position[:, None]) & (documents[:, None] == documents[None, :])
    rel_bias = bias_table[:, bucket_index(position[:, None] - position[None, :])]
    query_heads = queries.reshape(GROUP, HEADS, HEAD_DIM)
    key_heads = keys_all.reshape(GROUP, HEADS, HEAD_DIM)
    value_heads = values_all.reshape(GROUP, HEADS, HEAD_DIM)
    raw_scores = jnp.einsum('qhd,khd->hqk', query_heads, key_heads, precision=precise) * HEAD_DIM ** (-0.5)
    scores = jnp.where(allowed[None], low_back(raw_scores + rel_bias), NEGATIVE)
    probability = low(jax.nn.softmax(scores, axis=-1))
    attended = jnp.einsum('hqk,khd->qhd', probability, value_heads, precision=precise).reshape(GROUP, D)
    attended = low_back(low(attended))
    return stream + low_back(jnp.dot(attended, w_out, precision=precise))

def attention_all(stream, scales, weights, w_out, bias_table, bounds_all):

    def one_group(group_item):
        return attention_group(group_item[0], scales, weights, w_out, bias_table, group_item[1])
    grouped = stream.reshape(N_EXPERT, GROUP, D)
    return lax.map(jax.checkpoint(one_group), (grouped, bounds_all)).reshape(TOKENS, D)

def dense_layer(stream, scales, w_first, w_second):
    normed = low(normalize(stream, scales))
    pre_gate = low_back(jnp.dot(normed, w_first, precision=precise))
    hidden = low(jax.nn.gelu(pre_gate, approximate=True))
    return stream + low_back(jnp.dot(hidden, w_second, precision=precise))

def expert_layer(stream, scales, router_w, expert_first, expert_second, choice_ids):
    normed = low(normalize(stream, scales))
    logits = jnp.dot(normed, router_w, precision=precise)
    gate_weights = jax.nn.softmax(jnp.take_along_axis(logits, choice_ids, axis=1), axis=-1)
    device_count = N_EXPERT * N_DP
    per_device = choice_ids.reshape(device_count, TOK_DEV * 2)
    route_marks = (per_device[:, :, None] == jnp.arange(EXPERTS, dtype=jnp.int32)[None, None, :]).astype(jnp.int32)
    slot_ranks = lax.optimization_barrier(jnp.sum((jnp.cumsum(route_marks, axis=1) - route_marks) * route_marks, axis=2))
    buffer_rows = (jnp.arange(device_count, dtype=jnp.int32)[:, None] * CAP + slot_ranks).reshape(-1).astype(jnp.int32)
    flat_ids = choice_ids.reshape(-1)
    buffers = jnp.zeros((EXPERTS, device_count * CAP, D), jnp.float32).at[flat_ids, buffer_rows].set(jnp.repeat(normed, 2, axis=0))

    def one_expert(expert_item):
        rows_in, w_first, w_second = expert_item
        pre_gate = low_back(jnp.dot(rows_in, w_first, precision=precise))
        hidden = low(jax.nn.gelu(pre_gate, approximate=True))
        return low_back(low(jnp.dot(hidden, w_second, precision=precise)))
    produced = lax.map(jax.checkpoint(one_expert), (buffers, expert_first, expert_second))
    picked = produced[flat_ids, buffer_rows].reshape(TOKENS, 2, D)
    return stream + lax.optimization_barrier(jnp.sum(gate_weights[:, :, None] * picked, axis=1))

def forward(stream_all, gain_rows, qkv_all, out_all, table_flat, first_dense, second_dense, router_w, expert_first, expert_second, lengths, routes):
    bias_table = table_flat.reshape(2, HEADS, BUCKETS)
    results = []
    for micro_index in range(MICRO):
        stream = stream_all[micro_index]
        stream = attention_all(stream, gain_rows[0], qkv_all[0], out_all[0], bias_table[0], lengths[micro_index])
        stream = dense_layer(stream, gain_rows[1], first_dense, second_dense)
        stream = attention_all(stream, gain_rows[2], qkv_all[1], out_all[1], bias_table[1], lengths[micro_index])
        stream = expert_layer(stream, gain_rows[3], router_w, expert_first, expert_second, routes[micro_index])
        results.append(stream)
    return jnp.stack(results)

def reference(hidden_in, lengths, routes, norm_gains, qkv_weights, out_weights, rel_table, ffn_in, ffn_out, router, expert_in, expert_out, cotangent):

    def closed(stream_all, gain_rows, qkv_all, out_all, table_flat, first_dense, second_dense, router_w, expert_first, expert_second):
        return forward(stream_all, gain_rows, qkv_all, out_all, table_flat, first_dense, second_dense, router_w, expert_first, expert_second, lengths, routes)
    hidden_out, pullback = jax.vjp(closed, hidden_in.astype(jnp.float32), norm_gains.astype(jnp.float32), qkv_weights.astype(jnp.float32), out_weights.astype(jnp.float32), rel_table.astype(jnp.float32), ffn_in.astype(jnp.float32), ffn_out.astype(jnp.float32), router.astype(jnp.float32), expert_in.astype(jnp.float32), expert_out.astype(jnp.float32))
    grads = pullback(cotangent.astype(jnp.float32))
    return (hidden_out, grads[0], grads[1], grads[2], grads[3], grads[4], grads[5], grads[6], grads[7], grads[8], grads[9])
```

```python
import jax
import jax.numpy as jnp
from jax import lax
from jax.experimental import pallas as pl
from jax.experimental.pallas import tpu as pltpu
from jax.sharding import Mesh
from jax.sharding import PartitionSpec as P

WIDTH = 768
HEADS = 12
HEAD_DIM = 64
BUCKETS = 16
EXPERTS = 8
MICRO = 2
TOK = 72
ROWS = MICRO * TOK
GROUP = 1152
CAP = 20
FF = 3072
BLOCK = 128
SLOTS = 16
EPSILON = 1e-06
NEGATIVE = -1e30
SCALE = HEAD_DIM ** (-0.5)
LINE = ("y", "x")
ROW = ("z", "c")
ALL = ("z", "c", "y", "x")

bf16 = jnp.bfloat16
f32 = jnp.float32


def dot(a, b):
    return lax.dot_general(a, b, (((1,), (0,)), ((), ())), preferred_element_type=f32)


def dot_back(a, b):
    return lax.dot_general(a, b, (((1,), (1,)), ((), ())), preferred_element_type=f32)


def dot_outer(a, b):
    return lax.dot_general(a, b, (((0,), (0,)), ((), ())), preferred_element_type=f32)


def normalize(x, scales):
    inv = lax.rsqrt(jnp.mean(x * x, axis=-1, keepdims=True) + EPSILON)
    return (x * inv * scales).astype(bf16), inv


def normalize_back(grad, x, inv, scales):
    scaled = grad * scales
    mean = jnp.mean(scaled * x, axis=-1, keepdims=True)
    grad_x = inv * scaled - x * (inv * inv * inv) * mean
    grad_scales = jnp.sum(grad * x * inv, axis=0)
    return grad_x, grad_scales


def gelu(u):
    return jax.nn.gelu(u, approximate=True)


def forward_kernel(qk0_ref, qk1_ref, v_ref, bias_ref, start_ref, o_ref, lse_ref):
    for m, qk_ref in enumerate((qk0_ref, qk1_ref)):
        lanes = slice(m * HEAD_DIM, (m + 1) * HEAD_DIM)
        keys = qk_ref[:, HEAD_DIM:]
        values = v_ref[:, lanes]
        for i in range(GROUP // BLOCK):
            rows = slice(i * BLOCK, (i + 1) * BLOCK)
            width = (i + 1) * BLOCK
            scores = dot_back(qk_ref[rows, :HEAD_DIM], keys[:width])
            scores = scores + bias_ref[:, GROUP - width :]
            column = lax.broadcasted_iota(jnp.int32, (BLOCK, width), 1)
            scores = jnp.where(column >= start_ref[rows, m : m + 1], scores, NEGATIVE)
            peak = jnp.max(scores, axis=-1, keepdims=True)
            weights = jnp.exp(scores - peak)
            total = jnp.sum(weights, axis=-1, keepdims=True)
            probs = (weights * (1.0 / total)).astype(bf16)
            o_ref[rows, lanes] = dot(probs, values[:width]).astype(bf16)
            lse_ref[rows, m : m + 1] = peak + jnp.log(total)


def backward_kernel(
    qk0_ref, qk1_ref, v_ref, do_ref, bias_ref, start_ref, lse_ref,
    dqk0_ref, dqk1_ref, dv_ref, table_ref, dk_acc, dv_acc,
):
    table_ref[...] = jnp.zeros_like(table_ref)
    for m, (qk_ref, dqk_ref) in enumerate(((qk0_ref, dqk0_ref), (qk1_ref, dqk1_ref))):
        lanes = slice(m * HEAD_DIM, (m + 1) * HEAD_DIM)
        keys = qk_ref[:, HEAD_DIM:]
        values = v_ref[:, lanes]
        dk_acc[...] = jnp.zeros_like(dk_acc)
        dv_acc[...] = jnp.zeros_like(dv_acc)
        for i in range(GROUP // BLOCK):
            rows = slice(i * BLOCK, (i + 1) * BLOCK)
            width = (i + 1) * BLOCK
            query = qk_ref[rows, :HEAD_DIM]
            grad_o = do_ref[rows, lanes]
            scores = dot_back(query, keys[:width]) + bias_ref[:, GROUP - width :]
            column = lax.broadcasted_iota(jnp.int32, (BLOCK, width), 1)
            scores = jnp.where(column >= start_ref[rows, m : m + 1], scores, NEGATIVE)
            probs = jnp.exp(scores - lse_ref[rows, m : m + 1])
            grad_probs = dot_back(grad_o, values[:width])
            weighted = probs * grad_probs
            inner = jnp.sum(weighted, axis=-1, keepdims=True)
            grad_scores = (weighted - probs * inner).astype(bf16)
            table_ref[:, GROUP - width :] += grad_scores.astype(f32)
            dqk_ref[rows, :HEAD_DIM] = (dot(grad_scores, keys[:width]) * SCALE).astype(bf16)
            dk_acc[:width] += dot_outer(grad_scores, query)
            dv_acc[:width] += dot_outer(probs.astype(bf16), grad_o)
        dqk_ref[:, HEAD_DIM:] = dk_acc[...].astype(bf16)
        dv_ref[:, lanes] = dv_acc[...].astype(bf16)


LIMIT = pltpu.CompilerParams(vmem_limit_bytes=48 * 1024 * 1024)


def head_forward(qk0, qk1, v, bias, start):
    return pl.pallas_call(
        forward_kernel,
        out_shape=(
            jax.ShapeDtypeStruct((GROUP, 2 * HEAD_DIM), bf16),
            jax.ShapeDtypeStruct((GROUP, MICRO), f32),
        ),
        compiler_params=LIMIT,
        cost_estimate=pl.CostEstimate(
            flops=4 * MICRO * GROUP * GROUP * HEAD_DIM // 2,
            bytes_accessed=6 * GROUP * 256,
            transcendentals=MICRO * GROUP * GROUP // 2,
        ),
    )(qk0, qk1, v, bias, start)


def head_backward(qk0, qk1, v, grad_o, bias, start, lse):
    shape = jax.ShapeDtypeStruct((GROUP, 2 * HEAD_DIM), bf16)
    return pl.pallas_call(
        backward_kernel,
        out_shape=(shape, shape, shape, jax.ShapeDtypeStruct((BLOCK, GROUP), f32)),
        scratch_shapes=[pltpu.VMEM((GROUP, HEAD_DIM), f32), pltpu.VMEM((GROUP, HEAD_DIM), f32)],
        compiler_params=LIMIT,
        cost_estimate=pl.CostEstimate(
            flops=10 * MICRO * GROUP * GROUP * HEAD_DIM // 2,
            bytes_accessed=12 * GROUP * 256,
            transcendentals=MICRO * GROUP * GROUP // 2,
        ),
    )(qk0, qk1, v, grad_o, bias, start, lse)


def tile_distance():
    row = lax.broadcasted_iota(jnp.int32, (BLOCK, GROUP), 0)
    column = lax.broadcasted_iota(jnp.int32, (BLOCK, GROUP), 1)
    return row - column + (GROUP - BLOCK)


def bucket_starts():
    return [0, 1, 2, 3, 4, 5, 6, 7] + [2**t for t in range(3, 11)]


def bias_tile(entries):
    distance = tile_distance()
    result = jnp.full((BLOCK, GROUP), NEGATIVE, f32)
    for b, first in enumerate(bucket_starts()):
        result = jnp.where(distance >= first, entries[b], result)
    return result


def table_sums(tile):
    distance = tile_distance()
    above = [jnp.sum(jnp.where(distance >= first, tile, 0.0)) for first in bucket_starts()]
    above.append(jnp.zeros((), f32))
    return jnp.stack([above[b] - above[b + 1] for b in range(BUCKETS)])


def exchange(blocks, axes):
    return lax.all_to_all(blocks, axes, split_axis=0, concat_axis=0, tiled=True)


def pad_heads(blocks):
    return jnp.pad(blocks, ((0, SLOTS - HEADS), (0, 0), (0, 0)))


def by_head_single(values):
    parts = values.reshape(MICRO, TOK, HEADS, HEAD_DIM).transpose(2, 1, 0, 3)
    return parts.reshape(HEADS, TOK, MICRO * HEAD_DIM)


def from_head_single(blocks):
    parts = blocks.reshape(HEADS, TOK, MICRO, HEAD_DIM).transpose(2, 1, 0, 3)
    return parts.reshape(ROWS, WIDTH)


def send_heads(q, k, v):
    pair = jnp.stack([q.reshape(ROWS, HEADS, HEAD_DIM), k.reshape(ROWS, HEADS, HEAD_DIM)], axis=2)
    pair = pair.reshape(ROWS, HEADS, 2 * HEAD_DIM).transpose(1, 0, 2)
    blocks = exchange(pad_heads(jnp.concatenate([pair, by_head_single(v)], axis=1)), LINE)
    return tuple(
        blocks[:, j * TOK : (j + 1) * TOK].reshape(GROUP, 2 * HEAD_DIM) for j in range(3)
    )


def return_heads(dqk0, dqk1, dv):
    blocks = jnp.concatenate([a.reshape(SLOTS, TOK, 2 * HEAD_DIM) for a in (dqk0, dqk1, dv)], axis=1)
    blocks = exchange(blocks, LINE)[:HEADS]
    pair = blocks[:, :ROWS].reshape(HEADS, ROWS, 2, HEAD_DIM).transpose(2, 1, 0, 3)
    pair = pair.reshape(2, ROWS, WIDTH)
    return pair[0], pair[1], from_head_single(blocks[:, ROWS:])


def attend_forward(x, scales, weights, bias, start):
    normed, inv = normalize(x, scales)
    q = (dot(normed, weights[0]) * SCALE).astype(bf16)
    k = dot(normed, weights[1]).astype(bf16)
    v = dot(normed, weights[2]).astype(bf16)
    qk0, qk1, vv = send_heads(q, k, v)
    o, lse = head_forward(qk0, qk1, vv, bias, start)
    attended = from_head_single(exchange(o.reshape(SLOTS, TOK, 2 * HEAD_DIM), LINE)[:HEADS])
    return x + dot(attended, weights[3]), (normed, inv, qk0, qk1, vv, lse, attended)


def attend_backward(grad, x, scales, weights, bias, start, saved):
    normed, inv, qk0, qk1, vv, lse, attended = saved
    branch = grad.astype(bf16)
    grad_attended = dot_back(branch, weights[3]).astype(bf16)
    grad_o = exchange(pad_heads(by_head_single(grad_attended)), LINE).reshape(GROUP, 2 * HEAD_DIM)
    dqk0, dqk1, dv, tile = head_backward(qk0, qk1, vv, grad_o, bias, start, lse)
    dq, dk, dv = return_heads(dqk0, dqk1, dv)
    grad_normed = dot_back(dq, weights[0]) + dot_back(dk, weights[1]) + dot_back(dv, weights[2])
    grad_x, grad_scales = normalize_back(grad_normed, x, inv, scales)
    return grad + grad_x, grad_scales, branch, (dq, dk, dv), tile


def other_core(value):
    return lax.ppermute(value, "c", [(0, 1), (1, 0)])


def select_columns(core):
    out = lax.broadcasted_iota(jnp.int32, (WIDTH, WIDTH // 2), 1)
    source = lax.broadcasted_iota(jnp.int32, (WIDTH, WIDTH // 2), 0)
    line, rest = out // 24, out % 24
    z, i = rest // 6, rest % 6
    return (source == ((z * 2 + core) * 16 + line) * 6 + i).astype(bf16)


def pick(a, selector):
    return dot(a, selector).astype(bf16)


def on_device(
    hidden_in, lengths, routes, norm_gains, qkv_weights, out_weights, rel_table,
    ffn_in, ffn_out, router, expert_in, expert_out, cotangent,
):
    core = lax.axis_index("c")
    line_rank = lax.axis_index("y") * 4 + lax.axis_index("x")

    first_pack = jnp.concatenate([qkv_weights[0], out_weights[:1]], axis=0)
    second_pack = jnp.concatenate(
        [
            ffn_in.reshape(6, 4, WIDTH).transpose(1, 0, 2),
            ffn_out.reshape(4, 6, WIDTH),
            qkv_weights[1],
            out_weights[1:],
        ],
        axis=0,
    )
    first = lax.all_gather(first_pack, ALL, axis=1, tiled=True)
    second = lax.all_gather(second_pack, ALL, axis=1, tiled=True)
    w_expert_in = lax.all_gather(expert_in[0], LINE, axis=0, tiled=True)
    w_expert_out = lax.all_gather(expert_out[0], LINE, axis=0, tiled=True)
    w_in = [second[j] for j in range(4)]
    w_out = second[4:8].reshape(4, 128, 6, WIDTH).transpose(1, 0, 2, 3).reshape(FF, WIDTH)
    weights_one = second[8:]

    small = jnp.concatenate([norm_gains.reshape(24), router.reshape(48), rel_table])
    small = jnp.pad(small, (0, 128 - 75))[None, None, :]
    small = jnp.broadcast_to(small, (SLOTS, 8, 128))
    small = exchange(small, LINE).reshape(1, 128, 128)
    small = exchange(jnp.broadcast_to(small, (EXPERTS, 128, 128)), ROW)
    small = small.reshape(128, 8, 128)[:, 0]
    gains = small[:, :24].reshape(128, 4, 6).transpose(1, 0, 2).reshape(4, WIDTH).astype(f32)
    w_router = small[:, 24:72].reshape(WIDTH, EXPERTS)
    table = small[:, 72:75].reshape(2, HEADS, BUCKETS).astype(f32)
    head = jnp.minimum(line_rank, HEADS - 1)
    entries = lax.dynamic_index_in_dim(table, head, axis=1, keepdims=False)
    bias = [bias_tile(entries[layer]) for layer in range(2)]

    ends = jnp.cumsum(lengths[:, 0], axis=1)
    position = jnp.arange(GROUP, dtype=jnp.int32)[:, None, None]
    start = jnp.max(jnp.where(position >= ends[None], ends[None], 0), axis=2)

    x0 = hidden_in.reshape(ROWS, WIDTH).astype(f32)
    x1, saved_one = attend_forward(x0, gains[0], first, bias[0], start)
    c, inv_c = normalize(x1, gains[1])
    u = jnp.concatenate([dot(c, w) for w in w_in], axis=1)
    h = gelu(u).astype(bf16)
    x2 = x1 + dot(h, w_out)
    x3, saved_three = attend_forward(x2, gains[2], weights_one, bias[1], start)

    e, inv_e = normalize(x3, gains[3])
    logits = dot(e, w_router)
    choice = routes.reshape(ROWS, 2)
    marks = (choice[:, :, None] == jnp.arange(EXPERTS, dtype=jnp.int32)).astype(f32)
    chosen = jnp.sum(marks * logits[:, None, :], axis=-1)
    gates = jax.nn.softmax(chosen, axis=-1)
    pair_marks = marks.reshape(MICRO, TOK * 2, EXPERTS)
    earlier = jnp.cumsum(pair_marks, axis=1) - pair_marks
    slots = jnp.sum(earlier * pair_marks, axis=-1).astype(jnp.int32).reshape(ROWS, 2)
    micro = (jnp.arange(ROWS, dtype=jnp.int32) // TOK)[:, None]
    target = choice * 80 + micro * CAP + slots
    target_k = target.T
    row_id = jnp.arange(EXPERTS * 80, dtype=jnp.int32)
    place = [row_id[:, None] == target_k[k][None, :] for k in range(2)]
    place_back = [row_id[:, None] == target_k[k][None, :] + 40 for k in range(2)]
    scatter = jnp.concatenate([place[0] | place[1], place_back[0], place_back[1]], axis=1).astype(bf16)
    collect = jnp.concatenate([place_back[0] | place_back[1], place[0], place[1]], axis=1).astype(bf16)
    grad_four = cotangent.reshape(ROWS, WIDTH).astype(f32)
    picked_grads = [(gates[:, k : k + 1] * grad_four).astype(bf16) for k in range(2)]
    sent = dot(scatter, jnp.concatenate([e] + picked_grads, axis=0)).astype(bf16)
    arrived = exchange(sent.reshape(EXPERTS, 80, WIDTH), ROW)
    expert_rows = arrived[:, :40].reshape(320, WIDTH)
    grad_rows = arrived[:, 40:].reshape(320, WIDTH)
    ue = dot(expert_rows, w_expert_in)
    he, gelu_back = jax.vjp(gelu, ue)
    he = he.astype(bf16)
    ye = dot(he, w_expert_out).astype(bf16)
    due = gelu_back(dot_back(grad_rows, w_expert_out))[0].astype(bf16)
    grad_sent = dot_back(due, w_expert_in).astype(bf16)
    produced = jnp.concatenate([ye.reshape(EXPERTS, 40, WIDTH), grad_sent.reshape(EXPERTS, 40, WIDTH)], axis=1)
    returned = exchange(produced, ROW).reshape(EXPERTS * 80, WIDTH)
    collected = dot_outer(collect, returned)
    picked = [collected[ROWS : 2 * ROWS], collected[2 * ROWS :]]
    hidden_out = x3 + gates[:, :1] * picked[0] + gates[:, 1:] * picked[1]

    expert_parts = [
        dot_outer(expert_rows, due[:, j * WIDTH : (j + 1) * WIDTH]).astype(bf16).reshape(SLOTS, 48, WIDTH)
        for j in range(4)
    ] + [dot_outer(he, grad_rows).astype(bf16).reshape(SLOTS, 192, WIDTH)]
    expert_sum = lax.psum_scatter(
        jnp.concatenate(expert_parts, axis=1), LINE, scatter_dimension=0, tiled=False
    ).astype(f32)

    dgates = jnp.stack([jnp.sum(grad_four * p, axis=-1) for p in picked], axis=1)
    dchosen = gates * (dgates - jnp.sum(gates * dgates, axis=-1, keepdims=True))
    dlogits = jnp.sum(marks * dchosen[:, :, None], axis=1)
    grad_router = dot_outer(e, dlogits.astype(bf16))
    grad_e = collected[:ROWS] + dot_back(dlogits.astype(bf16), w_router)
    grad_x, gain_four = normalize_back(grad_e, x3, inv_e, gains[3])
    grad_three = grad_four + grad_x

    selector = select_columns(core)
    selector_other = select_columns(1 - core)

    def share(a, b):
        mine, theirs = pick(a, selector), pick(a, selector_other)
        got = other_core(jnp.concatenate([theirs, b], axis=1))
        return (
            jnp.concatenate([mine, got[:, : WIDTH // 2]], axis=0),
            jnp.concatenate([b, got[:, WIDTH // 2 :]], axis=0),
        )

    def chunks(a, b):
        return [
            dot_outer(a, b[:, j * WIDTH : (j + 1) * WIDTH]).astype(bf16).reshape(SLOTS, 24, WIDTH)
            for j in range(b.shape[1] // WIDTH)
        ]

    grad_two, gain_three, branch_three, heads_three, tile_three = attend_backward(
        grad_three, x2, gains[2], weights_one, bias[1], start, saved_three
    )
    parts = chunks(*share(saved_three[0], jnp.concatenate(heads_three, axis=1)))
    parts += chunks(*share(saved_three[6], branch_three))

    branch_two = grad_two.astype(bf16)
    grad_h = dot_back(branch_two, w_out)
    gelu_back_two = jax.vjp(gelu, u)[1]
    du = gelu_back_two(grad_h)[0].astype(bf16)
    grad_c = sum(dot_back(du[:, j * WIDTH : (j + 1) * WIDTH], w_in[j]) for j in range(4))
    grad_x, gain_two = normalize_back(grad_c, x1, inv_c, gains[1])
    grad_one = grad_two + grad_x
    parts += chunks(*share(c, du))
    halves = h.reshape(ROWS, 4, 2, FF // 8)
    mine = lax.dynamic_index_in_dim(halves, core, axis=2, keepdims=False).reshape(ROWS, FF // 2)
    theirs = lax.dynamic_index_in_dim(halves, 1 - core, axis=2, keepdims=False).reshape(ROWS, FF // 2)
    got = other_core(jnp.concatenate([theirs, branch_two], axis=1))
    mine = jnp.concatenate([mine, got[:, : FF // 2]], axis=0)
    second_grad = dot_outer(mine, jnp.concatenate([branch_two, got[:, FF // 2 :]], axis=0))
    second_grad = second_grad.astype(bf16).reshape(4, SLOTS, 24, WIDTH)
    parts += [second_grad[z] for z in range(4)]
    early_sum = lax.psum_scatter(
        jnp.concatenate(parts, axis=1), LINE, scatter_dimension=0, tiled=False
    )

    grad_zero, gain_one, branch_one, heads_one, tile_one = attend_backward(
        grad_one, x0, gains[0], first, bias[0], start, saved_one
    )
    late = chunks(*share(saved_one[0], jnp.concatenate(heads_one, axis=1)))
    late += chunks(*share(saved_one[6], branch_one))

    own_head = (jnp.arange(HEADS, dtype=jnp.int32) == line_rank).astype(f32)
    table_grad = jnp.stack([table_sums(tile_one), table_sums(tile_three)])
    table_grad = (own_head[None, :, None] * table_grad[:, None, :]).reshape(128, 3)
    gain_grad = jnp.stack([gain_one, gain_two, gain_three, gain_four])
    gain_grad = gain_grad.reshape(4, 128, 6).transpose(1, 0, 2).reshape(128, 24)
    tiny = jnp.concatenate([gain_grad, grad_router.reshape(128, 48), table_grad], axis=1)
    tiny = jnp.pad(tiny, ((0, 0), (0, 128 - 75))).reshape(4, 2, SLOTS, 128)
    tiny_mine = lax.dynamic_index_in_dim(tiny, core, axis=1, keepdims=False)
    tiny_theirs = lax.dynamic_index_in_dim(tiny, 1 - core, axis=1, keepdims=False)
    tiny_sum = tiny_mine + other_core(tiny_theirs)
    tiny_sum = tiny_sum.transpose(1, 0, 2).reshape(SLOTS, 1, 512)
    tiny_sum = jnp.pad(tiny_sum, ((0, 0), (0, 7), (0, 256))).astype(bf16)
    late_blocks = exchange(jnp.concatenate(late + [tiny_sum], axis=1), LINE)
    late_sum = jnp.sum(late_blocks.astype(f32), axis=0)

    tiny_rows = late_sum[96, :512].reshape(4, 1, 128)
    tiny_rows = jnp.pad(tiny_rows, ((0, 0), (0, 7), (0, WIDTH - 128)))
    late_rows = late_sum[:96].reshape(4, 4, 6, WIDTH)
    early = early_sum.astype(f32)
    early_rows = early[:192].reshape(8, 4, 6, WIDTH)
    ffn_out_rows = early[192:].reshape(4, 24, WIDTH)
    six = jnp.concatenate([late_rows, early_rows], axis=0).transpose(1, 0, 2, 3).reshape(4, 72, WIDTH)
    last = exchange(jnp.concatenate([six, ffn_out_rows, tiny_rows], axis=1).astype(bf16), ("z",))
    last = jnp.sum(last.astype(f32), axis=0)
    six = last[:72].reshape(12, 6, WIDTH)
    tiny = last[96, :75]
    out_shape = hidden_in.shape
    return (
        hidden_out.reshape(out_shape),
        grad_zero.reshape(out_shape),
        tiny[:24].reshape(4, 6),
        jnp.stack([six[0:3], six[4:7]]),
        jnp.stack([six[3], six[7]]),
        tiny[72:75],
        six[8:12].transpose(1, 0, 2).reshape(6, FF),
        last[72:96],
        tiny[24:72].reshape(6, EXPERTS),
        expert_sum[:192].reshape(4, 48, WIDTH).transpose(1, 0, 2).reshape(1, 48, FF),
        expert_sum[192:].reshape(1, 192, WIDTH),
    )


def solution(mesh):
    fine = Mesh(mesh.devices.reshape(4, 2, 4, 4), ALL)
    return jax.shard_map(
        on_device,
        mesh=fine,
        in_specs=(
            P(None, ALL, None),
            P(None, ROW, None),
            P(None, ALL, None),
            P(None, ALL),
            P(None, None, ALL, None),
            P(None, ALL, None),
            P(ALL),
            P(ALL, None),
            P(ALL, None),
            P(ALL, None),
            P(ROW, LINE, None),
            P(ROW, LINE, None),
            P(None, ALL, None),
        ),
        out_specs=(
            P(None, ALL, None),
            P(None, ALL, None),
            P(None, ALL),
            P(None, None, ALL, None),
            P(None, ALL, None),
            P(ALL),
            P(ALL, None),
            P(ALL, None),
            P(ALL, None),
            P(ROW, LINE, None),
            P(ROW, LINE, None),
        ),
        check_vma=False,
    )
```

```python
import jax
import jax.numpy as jnp
from jax import lax
from jax.experimental import pallas as pl
from jax.experimental.pallas import tpu as pltpu
from jax.sharding import Mesh
from jax.sharding import PartitionSpec as P

WIDTH = 768
HEADS = 12
HEAD_DIM = 64
BUCKETS = 16
EXPERTS = 8
MICRO = 2
TOK = 72
ROWS = MICRO * TOK
GROUP = 1152
CAP = 20
FF = 3072
BLOCK = 128
SLOTS = 16
EPSILON = 1e-06
NEGATIVE = -1e30
SCALE = HEAD_DIM ** (-0.5)
LINE = ("y", "x")
ROW = ("z", "c")
ALL = ("z", "c", "y", "x")

bf16 = jnp.bfloat16
f32 = jnp.float32


def dot(a, b):
    return lax.dot_general(a, b, (((1,), (0,)), ((), ())), preferred_element_type=f32)


def dot_back(a, b):
    return lax.dot_general(a, b, (((1,), (1,)), ((), ())), preferred_element_type=f32)


def dot_outer(a, b):
    return lax.dot_general(a, b, (((0,), (0,)), ((), ())), preferred_element_type=f32)


def normalize(x, scales):
    inv = lax.rsqrt(jnp.mean(x * x, axis=-1, keepdims=True) + EPSILON)
    return (x * inv * scales).astype(bf16), inv


def normalize_back(grad, x, inv, scales):
    scaled = grad * scales
    mean = jnp.mean(scaled * x, axis=-1, keepdims=True)
    grad_x = inv * scaled - x * (inv * inv * inv) * mean
    grad_scales = jnp.sum(grad * x * inv, axis=0)
    return grad_x, grad_scales


def gelu(u):
    return jax.nn.gelu(u, approximate=True)


def forward_kernel(qk0_ref, qk1_ref, v_ref, bias_ref, start_ref, o_ref, lse_ref):
    for m, qk_ref in enumerate((qk0_ref, qk1_ref)):
        lanes = slice(m * HEAD_DIM, (m + 1) * HEAD_DIM)
        keys = qk_ref[:, HEAD_DIM:]
        values = v_ref[:, lanes]
        for i in range(GROUP // BLOCK):
            rows = slice(i * BLOCK, (i + 1) * BLOCK)
            width = (i + 1) * BLOCK
            scores = dot_back(qk_ref[rows, :HEAD_DIM], keys[:width])
            scores = scores + bias_ref[:, GROUP - width :]
            column = lax.broadcasted_iota(jnp.int32, (BLOCK, width), 1)
            scores = jnp.where(column >= start_ref[rows, m : m + 1], scores, NEGATIVE)
            peak = jnp.max(scores, axis=-1, keepdims=True)
            weights = jnp.exp(scores - peak)
            total = jnp.sum(weights, axis=-1, keepdims=True)
            probs = (weights * (1.0 / total)).astype(bf16)
            o_ref[rows, lanes] = dot(probs, values[:width]).astype(bf16)
            lse_ref[rows, m : m + 1] = peak + jnp.log(total)


def backward_kernel(
    qk0_ref, qk1_ref, v_ref, do_ref, bias_ref, start_ref, lse_ref,
    dqk0_ref, dqk1_ref, dv_ref, table_ref, dk_acc, dv_acc,
):
    table_ref[...] = jnp.zeros_like(table_ref)
    for m, (qk_ref, dqk_ref) in enumerate(((qk0_ref, dqk0_ref), (qk1_ref, dqk1_ref))):
        lanes = slice(m * HEAD_DIM, (m + 1) * HEAD_DIM)
        keys = qk_ref[:, HEAD_DIM:]
        values = v_ref[:, lanes]
        dk_acc[...] = jnp.zeros_like(dk_acc)
        dv_acc[...] = jnp.zeros_like(dv_acc)
        for i in range(GROUP // BLOCK):
            rows = slice(i * BLOCK, (i + 1) * BLOCK)
            width = (i + 1) * BLOCK
            query = qk_ref[rows, :HEAD_DIM]
            grad_o = do_ref[rows, lanes]
            scores = dot_back(query, keys[:width]) + bias_ref[:, GROUP - width :]
            column = lax.broadcasted_iota(jnp.int32, (BLOCK, width), 1)
            scores = jnp.where(column >= start_ref[rows, m : m + 1], scores, NEGATIVE)
            probs = jnp.exp(scores - lse_ref[rows, m : m + 1])
            grad_probs = dot_back(grad_o, values[:width])
            weighted = probs * grad_probs
            inner = jnp.sum(weighted, axis=-1, keepdims=True)
            grad_scores = (weighted - probs * inner).astype(bf16)
            table_ref[:, GROUP - width :] += grad_scores.astype(f32)
            dqk_ref[rows, :HEAD_DIM] = (dot(grad_scores, keys[:width]) * SCALE).astype(bf16)
            dk_acc[:width] += dot_outer(grad_scores, query)
            dv_acc[:width] += dot_outer(probs.astype(bf16), grad_o)
        dqk_ref[:, HEAD_DIM:] = dk_acc[...].astype(bf16)
        dv_ref[:, lanes] = dv_acc[...].astype(bf16)


LIMIT = pltpu.CompilerParams(vmem_limit_bytes=48 * 1024 * 1024)


def head_forward(qk0, qk1, v, bias, start):
    return pl.pallas_call(
        forward_kernel,
        out_shape=(
            jax.ShapeDtypeStruct((GROUP, 2 * HEAD_DIM), bf16),
            jax.ShapeDtypeStruct((GROUP, MICRO), f32),
        ),
        compiler_params=LIMIT,
        cost_estimate=pl.CostEstimate(
            flops=4 * MICRO * GROUP * GROUP * HEAD_DIM // 2,
            bytes_accessed=6 * GROUP * 256,
            transcendentals=MICRO * GROUP * GROUP // 2,
        ),
    )(qk0, qk1, v, bias, start)


def head_backward(qk0, qk1, v, grad_o, bias, start, lse):
    shape = jax.ShapeDtypeStruct((GROUP, 2 * HEAD_DIM), bf16)
    return pl.pallas_call(
        backward_kernel,
        out_shape=(shape, shape, shape, jax.ShapeDtypeStruct((BLOCK, GROUP), f32)),
        scratch_shapes=[pltpu.VMEM((GROUP, HEAD_DIM), f32), pltpu.VMEM((GROUP, HEAD_DIM), f32)],
        compiler_params=LIMIT,
        cost_estimate=pl.CostEstimate(
            flops=10 * MICRO * GROUP * GROUP * HEAD_DIM // 2,
            bytes_accessed=12 * GROUP * 256,
            transcendentals=MICRO * GROUP * GROUP // 2,
        ),
    )(qk0, qk1, v, grad_o, bias, start, lse)


def tile_distance():
    row = lax.broadcasted_iota(jnp.int32, (BLOCK, GROUP), 0)
    column = lax.broadcasted_iota(jnp.int32, (BLOCK, GROUP), 1)
    return row - column + (GROUP - BLOCK)


def bucket_starts():
    return [0, 1, 2, 3, 4, 5, 6, 7] + [2**t for t in range(3, 11)]


def bias_tile(entries):
    distance = tile_distance()
    result = jnp.full((BLOCK, GROUP), NEGATIVE, f32)
    for b, first in enumerate(bucket_starts()):
        result = jnp.where(distance >= first, entries[b], result)
    return result


def table_sums(tile):
    distance = tile_distance()
    first = jnp.array(bucket_starts(), jnp.int32)[:, None, None]
    last = jnp.array(bucket_starts()[1:] + [GROUP], jnp.int32)[:, None, None]
    inside = (distance[None] >= first) & (distance[None] < last)
    return jnp.sum(jnp.where(inside, tile[None], 0.0), axis=(1, 2))


def exchange(blocks, axes):
    return lax.all_to_all(blocks, axes, split_axis=0, concat_axis=0, tiled=True)


def pad_heads(blocks):
    return jnp.pad(blocks, ((0, SLOTS - HEADS), (0, 0), (0, 0)))


def by_head_single(values):
    parts = values.reshape(MICRO, TOK, HEADS, HEAD_DIM).transpose(2, 1, 0, 3)
    return parts.reshape(HEADS, TOK, MICRO * HEAD_DIM)


def from_head_single(blocks):
    parts = blocks.reshape(HEADS, TOK, MICRO, HEAD_DIM).transpose(2, 1, 0, 3)
    return parts.reshape(ROWS, WIDTH)


def send_heads(q, k, v):
    pair = jnp.stack([q.reshape(ROWS, HEADS, HEAD_DIM), k.reshape(ROWS, HEADS, HEAD_DIM)], axis=2)
    pair = pair.reshape(ROWS, HEADS, 2 * HEAD_DIM).transpose(1, 0, 2)
    blocks = exchange(pad_heads(jnp.concatenate([pair, by_head_single(v)], axis=1)), LINE)
    return tuple(
        blocks[:, j * TOK : (j + 1) * TOK].reshape(GROUP, 2 * HEAD_DIM) for j in range(3)
    )


def return_heads(dqk0, dqk1, dv):
    blocks = jnp.concatenate([a.reshape(SLOTS, TOK, 2 * HEAD_DIM) for a in (dqk0, dqk1, dv)], axis=1)
    blocks = exchange(blocks, LINE)[:HEADS]
    pair = blocks[:, :ROWS].reshape(HEADS, ROWS, 2, HEAD_DIM).transpose(2, 1, 0, 3)
    pair = pair.reshape(2, ROWS, WIDTH)
    return pair[0], pair[1], from_head_single(blocks[:, ROWS:])


def spread_matrix():
    out = lax.broadcasted_iota(jnp.int32, (WIDTH, 1024), 1)
    source = lax.broadcasted_iota(jnp.int32, (WIDTH, 1024), 0)
    return ((out % 8 < 6) & (source == out // 8 * 6 + out % 8)).astype(bf16)


def spread(values, places):
    return dot(values, places).astype(bf16)


def gather_back(values, places):
    return dot_back(values.astype(bf16), places)


def attend_forward(x, scales, w_qkv, w_out, places, bias, start):
    normed, inv = normalize(x, scales)
    qkv = dot(spread(normed, places), w_qkv)
    q = (qkv[:, :WIDTH] * SCALE).astype(bf16)
    k = qkv[:, WIDTH : 2 * WIDTH].astype(bf16)
    v = qkv[:, 2 * WIDTH :].astype(bf16)
    qk0, qk1, vv = send_heads(q, k, v)
    o, lse = head_forward(qk0, qk1, vv, bias, start)
    attended = from_head_single(exchange(o.reshape(SLOTS, TOK, 2 * HEAD_DIM), LINE)[:HEADS])
    x = x + dot(spread(attended, places), w_out)
    return x, (normed, inv, qk0, qk1, vv, lse, attended)


def attend_backward(grad, x, scales, w_qkv, w_out, places, bias, start, saved):
    normed, inv, qk0, qk1, vv, lse, attended = saved
    branch = grad.astype(bf16)
    grad_attended = gather_back(dot_back(branch, w_out), places).astype(bf16)
    grad_o = exchange(pad_heads(by_head_single(grad_attended)), LINE).reshape(GROUP, 2 * HEAD_DIM)
    dqk0, dqk1, dv, tile = head_backward(qk0, qk1, vv, grad_o, bias, start, lse)
    heads = jnp.concatenate(return_heads(dqk0, dqk1, dv), axis=1)
    grad_normed = gather_back(dot_back(heads, w_qkv), places)
    grad_x, grad_scales = normalize_back(grad_normed, x, inv, scales)
    return grad + grad_x, grad_scales, branch, heads, tile


def other_core(value):
    return lax.ppermute(value, "c", [(0, 1), (1, 0)])


def select_columns(core, line_first):
    out = lax.broadcasted_iota(jnp.int32, (WIDTH, WIDTH // 2), 1)
    source = lax.broadcasted_iota(jnp.int32, (WIDTH, WIDTH // 2), 0)
    outer, i = out // 6, out % 6
    z, line = (outer % 4, outer // 4) if line_first else (outer // SLOTS, outer % SLOTS)
    return (source == ((z * 2 + core) * SLOTS + line) * 6 + i).astype(bf16)


def pick(a, selector):
    return dot(a, selector).astype(bf16)


def on_device(
    hidden_in, lengths, routes, norm_gains, qkv_weights, out_weights, rel_table,
    ffn_in, ffn_out, router, expert_in, expert_out, cotangent,
):
    core = lax.axis_index("c")
    line_rank = lax.axis_index("y") * 4 + lax.axis_index("x")

    places = spread_matrix()
    ffn_in_units = ffn_in.reshape(6, 128, 3, 8).transpose(0, 2, 1, 3).reshape(6, FF)
    attention = [
        jnp.concatenate([qkv_weights[l, 0], qkv_weights[l, 1], qkv_weights[l, 2], out_weights[l]], axis=1)
        for l in range(2)
    ]
    first_pack = jnp.pad(jnp.concatenate([attention[0], ffn_in_units], axis=1), ((0, 2), (0, 0)))
    first_pack = jnp.concatenate([first_pack, ffn_out[:8], ffn_out[8:16], ffn_out[16:]], axis=1)
    second_pack = jnp.pad(attention[1], ((0, 2), (0, 0)))
    first = lax.all_gather(first_pack, ALL, axis=0, tiled=True)
    second = lax.all_gather(second_pack, ALL, axis=0, tiled=True)
    w_expert_in = lax.all_gather(expert_in[0], LINE, axis=0, tiled=True)
    w_expert_out = lax.all_gather(expert_out[0], LINE, axis=0, tiled=True)
    qkv_zero, out_zero = first[:, : 3 * WIDTH], first[:, 3 * WIDTH : 4 * WIDTH]
    qkv_one, out_one = second[:, : 3 * WIDTH], second[:, 3 * WIDTH :]
    w_in = first[:, 4 * WIDTH : 8 * WIDTH]
    w_out = [first[:, (8 + g) * WIDTH : (9 + g) * WIDTH] for g in range(3)]

    small = jnp.concatenate([norm_gains.reshape(24), router.reshape(48), rel_table])
    small = jnp.pad(small, (0, 128 - 75))[None, None, :]
    small = jnp.broadcast_to(small, (SLOTS, 8, 128))
    small = exchange(small, LINE).reshape(1, 128, 128)
    small = exchange(jnp.broadcast_to(small, (EXPERTS, 128, 128)), ROW)
    small = small.reshape(128, 8, 128)[:, 0]
    gains = small[:, :24].reshape(128, 4, 6).transpose(1, 0, 2).reshape(4, WIDTH).astype(f32)
    w_router = small[:, 24:72].reshape(WIDTH, EXPERTS)
    table = small[:, 72:75].reshape(2, HEADS, BUCKETS).astype(f32)
    head = jnp.minimum(line_rank, HEADS - 1)
    entries = lax.dynamic_index_in_dim(table, head, axis=1, keepdims=False)
    bias = [bias_tile(entries[layer]) for layer in range(2)]

    ends = jnp.cumsum(lengths[:, 0], axis=1)
    position = jnp.arange(GROUP, dtype=jnp.int32)[:, None, None]
    start = jnp.max(jnp.where(position >= ends[None], ends[None], 0), axis=2)

    x0 = hidden_in.reshape(ROWS, WIDTH).astype(f32)
    x1, saved_one = attend_forward(x0, gains[0], qkv_zero, out_zero, places, bias[0], start)
    c, inv_c = normalize(x1, gains[1])
    u = dot(spread(c, places), w_in)
    h = gelu(u).astype(bf16)
    x2 = x1 + sum(dot(h[:, g * 1024 : (g + 1) * 1024], w_out[g]) for g in range(3))
    x3, saved_three = attend_forward(x2, gains[2], qkv_one, out_one, places, bias[1], start)

    e, inv_e = normalize(x3, gains[3])
    logits = dot(e, w_router)
    choice = routes.reshape(ROWS, 2)
    marks = (choice[:, :, None] == jnp.arange(EXPERTS, dtype=jnp.int32)).astype(f32)
    chosen = jnp.sum(marks * logits[:, None, :], axis=-1)
    gates = jax.nn.softmax(chosen, axis=-1)
    pair_marks = marks.reshape(MICRO, TOK * 2, EXPERTS)
    earlier = jnp.cumsum(pair_marks, axis=1) - pair_marks
    slots = jnp.sum(earlier * pair_marks, axis=-1).astype(jnp.int32).reshape(ROWS, 2)
    micro = (jnp.arange(ROWS, dtype=jnp.int32) // TOK)[:, None]
    target = choice * 80 + micro * CAP + slots
    target_k = target.T
    row_id = jnp.arange(EXPERTS * 80, dtype=jnp.int32)
    place = [row_id[:, None] == target_k[k][None, :] for k in range(2)]
    place_back = [row_id[:, None] == target_k[k][None, :] + 40 for k in range(2)]
    scatter = jnp.concatenate([place[0] | place[1], place_back[0], place_back[1]], axis=1).astype(bf16)
    collect = jnp.concatenate([place_back[0] | place_back[1], place[0], place[1]], axis=1).astype(bf16)
    grad_four = cotangent.reshape(ROWS, WIDTH).astype(f32)
    picked_grads = [(gates[:, k : k + 1] * grad_four).astype(bf16) for k in range(2)]
    sent = dot(scatter, jnp.concatenate([e] + picked_grads, axis=0)).astype(bf16)
    arrived = exchange(sent.reshape(EXPERTS, 80, WIDTH), ROW)
    expert_rows = arrived[:, :40].reshape(320, WIDTH)
    grad_rows = arrived[:, 40:].reshape(320, WIDTH)
    ue = dot(expert_rows, w_expert_in)
    he, gelu_back = jax.vjp(gelu, ue)
    he = he.astype(bf16)
    ye = dot(he, w_expert_out).astype(bf16)
    due = gelu_back(dot_back(grad_rows, w_expert_out))[0].astype(bf16)
    grad_sent = dot_back(due, w_expert_in).astype(bf16)
    produced = jnp.concatenate([ye.reshape(EXPERTS, 40, WIDTH), grad_sent.reshape(EXPERTS, 40, WIDTH)], axis=1)
    returned = exchange(produced, ROW).reshape(EXPERTS * 80, WIDTH)
    collected = dot_outer(collect, returned)
    picked = [collected[ROWS : 2 * ROWS], collected[2 * ROWS :]]
    hidden_out = x3 + gates[:, :1] * picked[0] + gates[:, 1:] * picked[1]

    expert_parts = [
        dot_outer(expert_rows, due[:, j * WIDTH : (j + 1) * WIDTH]).astype(bf16).reshape(SLOTS, 48, WIDTH)
        for j in range(4)
    ] + [dot_outer(he, grad_rows).astype(bf16).reshape(SLOTS, 192, WIDTH)]

    dgates = jnp.stack([jnp.sum(grad_four * p, axis=-1) for p in picked], axis=1)
    dchosen = gates * (dgates - jnp.sum(gates * dgates, axis=-1, keepdims=True))
    dlogits = jnp.sum(marks * dchosen[:, :, None], axis=1)
    grad_router = dot_outer(e, dlogits.astype(bf16))
    grad_e = collected[:ROWS] + dot_back(dlogits.astype(bf16), w_router)
    grad_x, gain_four = normalize_back(grad_e, x3, inv_e, gains[3])
    grad_three = grad_four + grad_x


    def share(a, b, line_first):
        mine = pick(a, select_columns(core, line_first))
        theirs = pick(a, select_columns(1 - core, line_first))
        got = other_core(jnp.concatenate([theirs, b], axis=1))
        return (
            jnp.concatenate([mine, got[:, : WIDTH // 2]], axis=0),
            jnp.concatenate([b, got[:, WIDTH // 2 :]], axis=0),
        )

    def chunks(a, b, count):
        return [
            dot_outer(a, b[:, j * WIDTH : (j + 1) * WIDTH]).astype(bf16).reshape(count, -1, WIDTH)
            for j in range(b.shape[1] // WIDTH)
        ]

    grad_two, gain_three, branch_three, heads_three, tile_three = attend_backward(
        grad_three, x2, gains[2], qkv_one, out_one, places, bias[1], start, saved_three
    )
    parts = chunks(*share(saved_three[0], heads_three, True), SLOTS)
    parts += chunks(*share(saved_three[6], branch_three, True), SLOTS)

    branch_two = grad_two.astype(bf16)
    grad_h = jnp.concatenate([dot_back(branch_two, w) for w in w_out], axis=1)
    gelu_back_two = jax.vjp(gelu, u)[1]
    du = gelu_back_two(grad_h)[0].astype(bf16)
    grad_c = gather_back(dot_back(du, w_in), places)
    grad_x, gain_two = normalize_back(grad_c, x1, inv_c, gains[1])
    grad_one = grad_two + grad_x
    parts += chunks(*share(c, du, True), SLOTS)
    parts += chunks(*share(saved_one[6], grad_one.astype(bf16), True), SLOTS)
    halves = h.reshape(ROWS, 12, 2, BLOCK)
    mine = lax.dynamic_index_in_dim(halves, core, axis=2, keepdims=False).reshape(ROWS, FF // 2)
    theirs = lax.dynamic_index_in_dim(halves, 1 - core, axis=2, keepdims=False).reshape(ROWS, FF // 2)
    got = other_core(jnp.concatenate([theirs, branch_two], axis=1))
    mine = jnp.concatenate([mine, got[:, : FF // 2]], axis=0)
    second_grad = dot_outer(mine, jnp.concatenate([branch_two, got[:, FF // 2 :]], axis=0))
    second_grad = second_grad.astype(bf16).reshape(12, SLOTS, 8, WIDTH).transpose(1, 0, 2, 3)
    parts.append(second_grad.reshape(SLOTS, 96, WIDTH))
    early_sum = lax.optimization_barrier(
        lax.psum_scatter(
            jnp.concatenate(parts + expert_parts, axis=1), LINE, scatter_dimension=0, tiled=False
        )
    )
    expert_sum = early_sum[312:]

    grad_zero, gain_one, branch_one, heads_one, tile_one = attend_backward(
        grad_one, x0, gains[0], qkv_zero, out_zero, places, bias[0], start, saved_one
    )
    late = chunks(*share(saved_one[0], heads_one, False), 64)

    own_head = (jnp.arange(HEADS, dtype=jnp.int32) == line_rank).astype(f32)
    table_grad = jnp.stack([table_sums(tile_one), table_sums(tile_three)])
    table_grad = (own_head[None, :, None] * table_grad[:, None, :]).reshape(128, 3)
    gain_grad = jnp.stack([gain_one, gain_two, gain_three, gain_four])
    gain_grad = gain_grad.reshape(4, 128, 6).transpose(1, 0, 2).reshape(128, 24)
    tiny = jnp.concatenate([gain_grad, grad_router.reshape(128, 48), table_grad], axis=1)
    tiny = jnp.pad(tiny, ((0, 0), (0, 128 - 75))).reshape(4, 2, SLOTS, 128)
    tiny_mine = lax.dynamic_index_in_dim(tiny, core, axis=1, keepdims=False)
    tiny_theirs = lax.dynamic_index_in_dim(tiny, 1 - core, axis=1, keepdims=False)
    tiny_sum = tiny_mine + other_core(tiny_theirs)
    tiny_sum = jnp.pad(tiny_sum.reshape(64, 1, 128), ((0, 0), (0, 5), (0, WIDTH - 128)))
    late_blocks = exchange(jnp.concatenate(late + [tiny_sum.astype(bf16)], axis=1), ("z", "y", "x"))
    late_sum = jnp.sum(late_blocks.astype(f32), axis=0)
    tiny = late_sum[18, :75]

    early_rows = early_sum[:216].reshape(9, 4, 6, WIDTH).transpose(1, 0, 2, 3).reshape(4, 54, WIDTH)
    ffn_out_rows = early_sum[216:312].reshape(3, 4, 8, WIDTH).transpose(1, 0, 2, 3).reshape(4, 24, WIDTH)
    last = jnp.concatenate([ffn_out_rows, early_rows], axis=1)
    last = exchange(jnp.pad(last, ((0, 0), (0, 2), (0, 0))), ("z",))
    last = jnp.sum(last.astype(f32), axis=0)
    six = last[24:78].reshape(9, 6, WIDTH)
    ffn_in_part = six[4:8].transpose(1, 0, 2).reshape(6, 3, 128, 8).transpose(0, 2, 1, 3)
    out_shape = hidden_in.shape
    return (
        hidden_out.reshape(out_shape),
        grad_zero.reshape(out_shape),
        tiny[:24].reshape(4, 6),
        jnp.stack([late_sum[:18].reshape(3, 6, WIDTH), six[0:3]]),
        jnp.stack([six[8], six[3]]),
        tiny[72:75],
        ffn_in_part.reshape(6, FF),
        last[:24],
        tiny[24:72].reshape(6, EXPERTS),
        expert_sum[:192].astype(f32).reshape(4, 48, WIDTH).transpose(1, 0, 2).reshape(1, 48, FF),
        expert_sum[192:].astype(f32).reshape(1, 192, WIDTH),
    )


def solution(mesh):
    fine = Mesh(mesh.devices.reshape(4, 2, 4, 4), ALL)
    return jax.shard_map(
        on_device,
        mesh=fine,
        in_specs=(
            P(None, ALL, None),
            P(None, ROW, None),
            P(None, ALL, None),
            P(None, ALL),
            P(None, None, ALL, None),
            P(None, ALL, None),
            P(ALL),
            P(ALL, None),
            P(ALL, None),
            P(ALL, None),
            P(ROW, LINE, None),
            P(ROW, LINE, None),
            P(None, ALL, None),
        ),
        out_specs=(
            P(None, ALL, None),
            P(None, ALL, None),
            P(None, ALL),
            P(None, None, ALL, None),
            P(None, ALL, None),
            P(ALL),
            P(ALL, None),
            P(ALL, None),
            P(ALL, None),
            P(ROW, LINE, None),
            P(ROW, LINE, None),
        ),
        check_vma=False,
    )
```

```python
import jax
import jax.numpy as jnp
from jax import lax
from jax.experimental import pallas as pl
from jax.experimental.pallas import tpu as pltpu
from jax.sharding import Mesh
from jax.sharding import PartitionSpec as P

WIDTH = 768
HEADS = 12
HEAD_DIM = 64
BUCKETS = 16
EXPERTS = 8
MICRO = 2
TOK = 72
ROWS = MICRO * TOK
GROUP = 1152
CAP = 20
FF = 3072
BLOCK = 128
SLOTS = 16
EPSILON = 1e-06
NEGATIVE = -1e30
SCALE = HEAD_DIM ** (-0.5)
LINE = ("y", "x")
ROW = ("z", "c")
ALL = ("z", "c", "y", "x")

bf16 = jnp.bfloat16
f32 = jnp.float32


def dot(a, b):
    return lax.dot_general(a, b, (((1,), (0,)), ((), ())), preferred_element_type=f32)


def dot_back(a, b):
    return lax.dot_general(a, b, (((1,), (1,)), ((), ())), preferred_element_type=f32)


def dot_outer(a, b):
    return lax.dot_general(a, b, (((0,), (0,)), ((), ())), preferred_element_type=f32)


def normalize(x, scales):
    inv = lax.rsqrt(jnp.mean(x * x, axis=-1, keepdims=True) + EPSILON)
    return (x * inv * scales).astype(bf16), inv


def normalize_back(grad, x, inv, scales):
    scaled = grad * scales
    mean = jnp.mean(scaled * x, axis=-1, keepdims=True)
    grad_x = inv * scaled - x * (inv * inv * inv) * mean
    grad_scales = jnp.sum(grad * x * inv, axis=0)
    return grad_x, grad_scales


def gelu(u):
    return jax.nn.gelu(u, approximate=True)


LIMIT = pltpu.CompilerParams(vmem_limit_bytes=48 * 1024 * 1024)


def split_blocks(blocks_ref, targets):
    whole = blocks_ref[...].astype(f32)
    for j, target in enumerate(targets):
        target[...] = whole[:, j * TOK : (j + 1) * TOK].reshape(GROUP, 2 * HEAD_DIM).astype(bf16)


def forward_kernel(blocks_ref, bias_ref, start_ref, o_ref, lse_ref, qk0_ref, qk1_ref, v_ref):
    split_blocks(blocks_ref, (qk0_ref, qk1_ref, v_ref))
    for m, qk_ref in enumerate((qk0_ref, qk1_ref)):
        lanes = slice(m * HEAD_DIM, (m + 1) * HEAD_DIM)
        keys = qk_ref[:, HEAD_DIM:]
        values = v_ref[:, lanes]
        for i in range(GROUP // BLOCK):
            rows = slice(i * BLOCK, (i + 1) * BLOCK)
            width = (i + 1) * BLOCK
            scores = dot_back(qk_ref[rows, :HEAD_DIM], keys[:width])
            scores = scores + bias_ref[:, GROUP - width :]
            column = lax.broadcasted_iota(jnp.int32, (BLOCK, width), 1)
            scores = jnp.where(column >= start_ref[rows, m : m + 1], scores, NEGATIVE)
            peak = jnp.max(scores, axis=-1, keepdims=True)
            weights = jnp.exp(scores - peak)
            total = jnp.sum(weights, axis=-1, keepdims=True)
            probs = (weights * (1.0 / total)).astype(bf16)
            o_ref[rows, lanes] = dot(probs, values[:width]).astype(bf16)
            lse_ref[rows, m : m + 1] = peak + jnp.log(total)


def backward_kernel(
    blocks_ref, do_ref, bias_ref, start_ref, lse_ref, grads_ref, table_ref,
    qk0_ref, qk1_ref, v_ref, dqk0_ref, dqk1_ref, dv_ref, dk_acc, dv_acc,
):
    split_blocks(blocks_ref, (qk0_ref, qk1_ref, v_ref))
    table_ref[...] = jnp.zeros_like(table_ref)
    for m, (qk_ref, dqk_ref) in enumerate(((qk0_ref, dqk0_ref), (qk1_ref, dqk1_ref))):
        lanes = slice(m * HEAD_DIM, (m + 1) * HEAD_DIM)
        keys = qk_ref[:, HEAD_DIM:]
        values = v_ref[:, lanes]
        dk_acc[...] = jnp.zeros_like(dk_acc)
        dv_acc[...] = jnp.zeros_like(dv_acc)
        for i in range(GROUP // BLOCK):
            rows = slice(i * BLOCK, (i + 1) * BLOCK)
            width = (i + 1) * BLOCK
            query = qk_ref[rows, :HEAD_DIM]
            grad_o = do_ref[rows, lanes]
            scores = dot_back(query, keys[:width]) + bias_ref[:, GROUP - width :]
            column = lax.broadcasted_iota(jnp.int32, (BLOCK, width), 1)
            scores = jnp.where(column >= start_ref[rows, m : m + 1], scores, NEGATIVE)
            probs = jnp.exp(scores - lse_ref[rows, m : m + 1])
            grad_probs = dot_back(grad_o, values[:width])
            weighted = probs * grad_probs
            inner = jnp.sum(weighted, axis=-1, keepdims=True)
            grad_scores = (weighted - probs * inner).astype(bf16)
            table_ref[:, GROUP - width :] += grad_scores.astype(f32)
            dqk_ref[rows, :HEAD_DIM] = dot(grad_scores, keys[:width]) * SCALE
            dk_acc[:width] += dot_outer(grad_scores, query)
            dv_acc[:width] += dot_outer(probs.astype(bf16), grad_o)
        dqk_ref[:, HEAD_DIM:] = dk_acc[...]
        dv_ref[:, lanes] = dv_acc[...]
    parts = [r[...].reshape(SLOTS, TOK, 2 * HEAD_DIM) for r in (dqk0_ref, dqk1_ref, dv_ref)]
    grads_ref[...] = jnp.concatenate(parts, axis=1).astype(bf16)


def swap(values):
    return pltpu.roll(values, HEAD_DIM, 1)


def low_half(rows):
    return lax.broadcasted_iota(jnp.int32, (rows, 2 * HEAD_DIM), 1) < HEAD_DIM


def interleave(first, second):
    low = low_half(first.shape[0])
    return jnp.where(low, first, swap(second)), jnp.where(low, swap(first), second)


def pair_lanes(pair, offset=0):
    return slice(offset + pair * 2 * HEAD_DIM, offset + (pair + 1) * 2 * HEAD_DIM)


def pack_qkv_kernel(qkv_ref, out_ref):
    for pair in range(HEADS // 2):
        q = qkv_ref[:, pair_lanes(pair)] * SCALE
        k = qkv_ref[:, pair_lanes(pair, WIDTH)]
        v = qkv_ref[:, pair_lanes(pair, 2 * WIDTH)]
        heads = interleave(q, k)
        values = interleave(v[:TOK], v[TOK:])
        for j in range(2):
            out_ref[2 * pair + j] = jnp.concatenate([heads[j], values[j]], axis=0).astype(bf16)
    for slot in range(HEADS, SLOTS):
        out_ref[slot] = jnp.zeros_like(out_ref[slot])


def unpack_qkv_kernel(in_ref, out_ref):
    for pair in range(HEADS // 2):
        even, odd = in_ref[2 * pair].astype(f32), in_ref[2 * pair + 1].astype(f32)
        q, k = interleave(even[:ROWS], odd[:ROWS])
        v = jnp.concatenate(interleave(even[ROWS:], odd[ROWS:]), axis=0)
        for j, value in enumerate((q, k, v)):
            out_ref[:, pair_lanes(pair, j * WIDTH)] = value.astype(bf16)


def pack_one_kernel(in_ref, out_ref):
    for pair in range(HEADS // 2):
        values = in_ref[:, pair_lanes(pair)]
        for j, value in enumerate(interleave(values[:TOK], values[TOK:])):
            out_ref[2 * pair + j] = value.astype(bf16)
    for slot in range(HEADS, SLOTS):
        out_ref[slot] = jnp.zeros_like(out_ref[slot])


def unpack_one_kernel(in_ref, out_ref):
    for pair in range(HEADS // 2):
        even, odd = in_ref[2 * pair].astype(f32), in_ref[2 * pair + 1].astype(f32)
        values = jnp.concatenate(interleave(even, odd), axis=0)
        out_ref[:, pair_lanes(pair)] = values.astype(bf16)


def repack(kernel, shape, values):
    return pl.pallas_call(
        kernel,
        out_shape=jax.ShapeDtypeStruct(shape, bf16),
        compiler_params=LIMIT,
        cost_estimate=pl.CostEstimate(flops=1000000, bytes_accessed=1500000, transcendentals=0),
    )(values)


def products_kernel(
    a_qkv, b_q, b_k, b_v, a_out, b_out, a_in, b_in0, b_in1, b_in2, b_in3, a_zero, b_zero, a_second, b_second,
    a_rows, b_due0, b_due1, b_due2, b_due3, a_hidden, b_rows, out_ref,
):
    def rows(a, b, count):
        return dot_outer(a[...], b[...]).reshape(SLOTS, count, -1)

    def put(first, parts):
        value = jnp.concatenate(parts, axis=1).astype(bf16)
        out_ref[:, first : first + value.shape[1]] = value

    put(0, [rows(a_qkv, b, 24) for b in (b_q, b_k, b_v)] + [rows(a_out, b_out, 24)])
    put(96, [rows(a_in, b, 24) for b in (b_in0, b_in1, b_in2, b_in3)])
    zero = rows(a_zero, b_zero, 24)
    put(192, [zero, jnp.zeros_like(zero[:, :8])])
    second = dot_outer(a_second[...], b_second[...]).reshape(12, SLOTS, 8, -1)
    put(224, [second[j] for j in range(12)])
    put(320, [rows(a_rows, b, 48) for b in (b_due0, b_due1, b_due2, b_due3)])
    put(512, [rows(a_hidden, b_rows, 192)])


def products(qkv, out, dense_in, zero, second, expert_in, expert_out):
    step = 256
    operands, specs = [], []

    def whole(a):
        operands.append(a)
        specs.append(pl.BlockSpec(a.shape, lambda n: (0, 0)))

    def columns(b, count):
        for j in range(count):
            operands.append(b)
            specs.append(pl.BlockSpec((b.shape[0], step), lambda n, j=j: (0, n + j * (WIDTH // step))))

    for (a, b), count in zip((qkv, out, dense_in, zero, second, expert_in, expert_out), (3, 1, 4, 1, 1, 4, 1)):
        whole(a)
        columns(b, count)
    return pl.pallas_call(
        products_kernel,
        grid=(WIDTH // step,),
        in_specs=specs,
        out_specs=pl.BlockSpec((SLOTS, 704, step), lambda n: (0, 0, n)),
        out_shape=jax.ShapeDtypeStruct((SLOTS, 704, WIDTH), bf16),
        compiler_params=LIMIT,
        cost_estimate=pl.CostEstimate(flops=5200000000, bytes_accessed=30000000, transcendentals=0),
    )(*operands)


def staging(dtype, count):
    return [pltpu.VMEM((GROUP, 2 * HEAD_DIM), dtype)] * count


def head_forward(blocks, bias, start):
    return pl.pallas_call(
        forward_kernel,
        out_shape=(
            jax.ShapeDtypeStruct((GROUP, 2 * HEAD_DIM), bf16),
            jax.ShapeDtypeStruct((GROUP, MICRO), f32),
        ),
        scratch_shapes=staging(bf16, 3),
        compiler_params=LIMIT,
        cost_estimate=pl.CostEstimate(
            flops=4 * MICRO * GROUP * GROUP * HEAD_DIM // 2,
            bytes_accessed=6 * GROUP * 256,
            transcendentals=MICRO * GROUP * GROUP // 2,
        ),
    )(blocks, bias, start)


def head_backward(blocks, grad_o, bias, start, lse):
    return pl.pallas_call(
        backward_kernel,
        out_shape=(
            jax.ShapeDtypeStruct((SLOTS, 3 * TOK, 2 * HEAD_DIM), bf16),
            jax.ShapeDtypeStruct((BLOCK, GROUP), f32),
        ),
        scratch_shapes=staging(bf16, 3)
        + staging(f32, 3)
        + [pltpu.VMEM((GROUP, HEAD_DIM), f32), pltpu.VMEM((GROUP, HEAD_DIM), f32)],
        compiler_params=LIMIT,
        cost_estimate=pl.CostEstimate(
            flops=10 * MICRO * GROUP * GROUP * HEAD_DIM // 2,
            bytes_accessed=12 * GROUP * 256,
            transcendentals=MICRO * GROUP * GROUP // 2,
        ),
    )(blocks, grad_o, bias, start, lse)


def tile_distance():
    row = lax.broadcasted_iota(jnp.int32, (BLOCK, GROUP), 0)
    column = lax.broadcasted_iota(jnp.int32, (BLOCK, GROUP), 1)
    return row - column + (GROUP - BLOCK)


def bucket_starts():
    return [0, 1, 2, 3, 4, 5, 6, 7] + [2**t for t in range(3, 11)]


def bias_tile(entries):
    distance = tile_distance()
    result = jnp.full((BLOCK, GROUP), NEGATIVE, f32)
    for b, first in enumerate(bucket_starts()):
        result = jnp.where(distance >= first, entries[b], result)
    return result


def table_sums(tile):
    distance = tile_distance()
    first = jnp.array(bucket_starts(), jnp.int32)[:, None, None]
    last = jnp.array(bucket_starts()[1:] + [GROUP], jnp.int32)[:, None, None]
    inside = (distance[None] >= first) & (distance[None] < last)
    return jnp.sum(jnp.where(inside, tile[None], 0.0), axis=(1, 2))


def exchange(blocks, axes):
    return lax.all_to_all(blocks, axes, split_axis=0, concat_axis=0, tiled=True)


def spread_matrix():
    out = lax.broadcasted_iota(jnp.int32, (WIDTH, 1024), 1)
    source = lax.broadcasted_iota(jnp.int32, (WIDTH, 1024), 0)
    return ((out % 8 < 6) & (source == out // 8 * 6 + out % 8)).astype(bf16)


def spread(values, places):
    return dot(values, places).astype(bf16)


def gather_back(values, places):
    return dot_back(values.astype(bf16), places)


HEAD_SHAPE = (SLOTS, 3 * TOK, 2 * HEAD_DIM)
ONE_SHAPE = (SLOTS, TOK, 2 * HEAD_DIM)


def attend_forward(x, scales, w_qkv, w_out, places, bias, start):
    normed, inv = normalize(x, scales)
    blocks = exchange(repack(pack_qkv_kernel, HEAD_SHAPE, dot(spread(normed, places), w_qkv)), LINE)
    o, lse = head_forward(blocks, bias, start)
    attended = repack(unpack_one_kernel, (ROWS, WIDTH), exchange(o.reshape(ONE_SHAPE), LINE))
    x = x + dot(spread(attended, places), w_out)
    return x, (normed, inv, blocks, lse, attended)


def attend_backward(grad, x, scales, w_qkv, w_out, places, bias, start, saved):
    normed, inv, blocks, lse, attended = saved
    branch = grad.astype(bf16)
    grad_attended = gather_back(dot_back(branch, w_out), places)
    grad_o = exchange(repack(pack_one_kernel, ONE_SHAPE, grad_attended), LINE)
    grad_heads, tile = head_backward(blocks, grad_o.reshape(GROUP, 2 * HEAD_DIM), bias, start, lse)
    heads = repack(unpack_qkv_kernel, (ROWS, 3 * WIDTH), exchange(grad_heads, LINE))
    grad_normed = gather_back(dot_back(heads, w_qkv), places)
    grad_x, grad_scales = normalize_back(grad_normed, x, inv, scales)
    return grad + grad_x, grad_scales, branch, heads, tile


def other_core(value):
    return lax.ppermute(value, "c", [(0, 1), (1, 0)])


def select_columns(core, line_first):
    out = lax.broadcasted_iota(jnp.int32, (WIDTH, WIDTH // 2), 1)
    source = lax.broadcasted_iota(jnp.int32, (WIDTH, WIDTH // 2), 0)
    outer, i = out // 6, out % 6
    z, line = (outer % 4, outer // 4) if line_first else (outer // SLOTS, outer % SLOTS)
    return (source == ((z * 2 + core) * SLOTS + line) * 6 + i).astype(bf16)


def pick(a, selector):
    return dot(a, selector).astype(bf16)


def on_device(
    hidden_in, lengths, routes, norm_gains, qkv_weights, out_weights, rel_table,
    ffn_in, ffn_out, router, expert_in, expert_out, cotangent,
):
    core = lax.axis_index("c")
    line_rank = lax.axis_index("y") * 4 + lax.axis_index("x")

    places = spread_matrix()
    ffn_in_units = ffn_in.reshape(6, 128, 3, 8).transpose(0, 2, 1, 3).reshape(6, FF)
    attention = [
        jnp.concatenate([qkv_weights[l, 0], qkv_weights[l, 1], qkv_weights[l, 2], out_weights[l]], axis=1)
        for l in range(2)
    ]
    pack = jnp.pad(jnp.concatenate(attention + [ffn_in_units], axis=1), ((0, 2), (0, 0)))
    pack = jnp.concatenate([pack, ffn_out[:8], ffn_out[8:16], ffn_out[16:]], axis=1)
    shared = lax.all_gather(pack, ALL, axis=0, tiled=True)
    w_expert_in = lax.all_gather(expert_in[0], LINE, axis=0, tiled=True)
    w_expert_out = lax.all_gather(expert_out[0], LINE, axis=0, tiled=True)
    qkv_zero, out_zero = shared[:, : 3 * WIDTH], shared[:, 3 * WIDTH : 4 * WIDTH]
    qkv_one, out_one = shared[:, 4 * WIDTH : 7 * WIDTH], shared[:, 7 * WIDTH : 8 * WIDTH]
    w_in = shared[:, 8 * WIDTH : 12 * WIDTH]
    w_out = [shared[:, (12 + g) * WIDTH : (13 + g) * WIDTH] for g in range(3)]

    small = jnp.concatenate([norm_gains.reshape(24), router.reshape(48), rel_table])
    small = jnp.pad(small, (0, 128 - 75))[None, None, :]
    small = jnp.broadcast_to(small, (SLOTS, 8, 128))
    small = exchange(small, LINE).reshape(1, 128, 128)
    small = exchange(jnp.broadcast_to(small, (EXPERTS, 128, 128)), ROW)
    small = small.reshape(128, 8, 128)[:, 0]
    gains = small[:, :24].reshape(128, 4, 6).transpose(1, 0, 2).reshape(4, WIDTH).astype(f32)
    w_router = small[:, 24:72].reshape(WIDTH, EXPERTS)
    table = small[:, 72:75].reshape(2, HEADS, BUCKETS).astype(f32)
    head = jnp.minimum(line_rank, HEADS - 1)
    entries = lax.dynamic_index_in_dim(table, head, axis=1, keepdims=False)
    bias = [bias_tile(entries[layer]) for layer in range(2)]

    ends = jnp.cumsum(lengths[:, 0], axis=1)
    position = jnp.arange(GROUP, dtype=jnp.int32)[:, None, None]
    start = jnp.max(jnp.where(position >= ends[None], ends[None], 0), axis=2)

    x0 = hidden_in.reshape(ROWS, WIDTH).astype(f32)
    x1, saved_one = attend_forward(x0, gains[0], qkv_zero, out_zero, places, bias[0], start)
    c, inv_c = normalize(x1, gains[1])
    u = dot(spread(c, places), w_in)
    h = gelu(u).astype(bf16)
    x2 = x1 + sum(dot(h[:, g * 1024 : (g + 1) * 1024], w_out[g]) for g in range(3))
    x3, saved_three = attend_forward(x2, gains[2], qkv_one, out_one, places, bias[1], start)

    e, inv_e = normalize(x3, gains[3])
    logits = dot(e, w_router)
    choice = routes.reshape(ROWS, 2)
    marks = (choice[:, :, None] == jnp.arange(EXPERTS, dtype=jnp.int32)).astype(f32)
    chosen = jnp.sum(marks * logits[:, None, :], axis=-1)
    gates = jax.nn.softmax(chosen, axis=-1)
    pair_marks = marks.reshape(MICRO, TOK * 2, EXPERTS)
    earlier = jnp.cumsum(pair_marks, axis=1) - pair_marks
    slots = jnp.sum(earlier * pair_marks, axis=-1).astype(jnp.int32).reshape(ROWS, 2)
    micro = (jnp.arange(ROWS, dtype=jnp.int32) // TOK)[:, None]
    target = choice * 80 + micro * CAP + slots
    target_k = target.T
    row_id = jnp.arange(EXPERTS * 80, dtype=jnp.int32)
    place = [row_id[:, None] == target_k[k][None, :] for k in range(2)]
    place_back = [row_id[:, None] == target_k[k][None, :] + 40 for k in range(2)]
    scatter = jnp.concatenate([place[0] | place[1], place_back[0], place_back[1]], axis=1).astype(bf16)
    collect = jnp.concatenate([place_back[0] | place_back[1], place[0], place[1]], axis=1).astype(bf16)
    grad_four = cotangent.reshape(ROWS, WIDTH).astype(f32)
    picked_grads = [(gates[:, k : k + 1] * grad_four).astype(bf16) for k in range(2)]
    sent = dot(scatter, jnp.concatenate([e] + picked_grads, axis=0)).astype(bf16)
    arrived = exchange(sent.reshape(EXPERTS, 80, WIDTH), ROW)
    expert_rows = arrived[:, :40].reshape(320, WIDTH)
    grad_rows = arrived[:, 40:].reshape(320, WIDTH)
    ue = dot(expert_rows, w_expert_in)
    he, gelu_back = jax.vjp(gelu, ue)
    he = he.astype(bf16)
    ye = dot(he, w_expert_out).astype(bf16)
    due = gelu_back(dot_back(grad_rows, w_expert_out))[0].astype(bf16)
    grad_sent = dot_back(due, w_expert_in).astype(bf16)
    produced = jnp.concatenate([ye.reshape(EXPERTS, 40, WIDTH), grad_sent.reshape(EXPERTS, 40, WIDTH)], axis=1)
    returned = exchange(produced, ROW).reshape(EXPERTS * 80, WIDTH)
    collected = dot_outer(collect, returned)
    picked = [collected[ROWS : 2 * ROWS], collected[2 * ROWS :]]
    hidden_out = x3 + gates[:, :1] * picked[0] + gates[:, 1:] * picked[1]

    dgates = jnp.stack([jnp.sum(grad_four * p, axis=-1) for p in picked], axis=1)
    dchosen = gates * (dgates - jnp.sum(gates * dgates, axis=-1, keepdims=True))
    dlogits = jnp.sum(marks * dchosen[:, :, None], axis=1)
    grad_router = dot_outer(e, dlogits.astype(bf16))
    grad_e = collected[:ROWS] + dot_back(dlogits.astype(bf16), w_router)
    grad_x, gain_four = normalize_back(grad_e, x3, inv_e, gains[3])
    grad_three = grad_four + grad_x


    def share(a, b, line_first):
        mine = pick(a, select_columns(core, line_first))
        theirs = pick(a, select_columns(1 - core, line_first))
        got = other_core(jnp.concatenate([theirs, b], axis=1))
        return (
            jnp.concatenate([mine, got[:, : WIDTH // 2]], axis=0),
            jnp.concatenate([b, got[:, WIDTH // 2 :]], axis=0),
        )

    def chunks(a, b, count):
        return [
            dot_outer(a, b[:, j * WIDTH : (j + 1) * WIDTH]).astype(bf16).reshape(count, -1, WIDTH)
            for j in range(b.shape[1] // WIDTH)
        ]

    grad_two, gain_three, branch_three, heads_three, tile_three = attend_backward(
        grad_three, x2, gains[2], qkv_one, out_one, places, bias[1], start, saved_three
    )
    pair_qkv = share(saved_three[0], heads_three, True)
    pair_out = share(saved_three[4], branch_three, True)

    branch_two = grad_two.astype(bf16)
    grad_h = jnp.concatenate([dot_back(branch_two, w) for w in w_out], axis=1)
    gelu_back_two = jax.vjp(gelu, u)[1]
    du = gelu_back_two(grad_h)[0].astype(bf16)
    grad_c = gather_back(dot_back(du, w_in), places)
    grad_x, gain_two = normalize_back(grad_c, x1, inv_c, gains[1])
    grad_one = grad_two + grad_x
    pair_in = share(c, du, True)
    pair_zero = share(saved_one[4], grad_one.astype(bf16), True)
    halves = h.reshape(ROWS, 12, 2, BLOCK)
    mine = lax.dynamic_index_in_dim(halves, core, axis=2, keepdims=False).reshape(ROWS, FF // 2)
    theirs = lax.dynamic_index_in_dim(halves, 1 - core, axis=2, keepdims=False).reshape(ROWS, FF // 2)
    got = other_core(jnp.concatenate([theirs, branch_two], axis=1))
    mine = jnp.concatenate([mine, got[:, : FF // 2]], axis=0)
    pair_second = (mine, jnp.concatenate([branch_two, got[:, FF // 2 :]], axis=0))
    summed = products(
        pair_qkv, pair_out, pair_in, pair_zero, pair_second, (expert_rows, due), (he, grad_rows)
    )
    early_sum = lax.optimization_barrier(
        lax.psum_scatter(summed, LINE, scatter_dimension=0, tiled=False)
    )
    expert_sum = early_sum[320:]

    grad_zero, gain_one, branch_one, heads_one, tile_one = attend_backward(
        grad_one, x0, gains[0], qkv_zero, out_zero, places, bias[0], start, saved_one
    )
    late = chunks(*share(saved_one[0], heads_one, False), 64)

    own_head = (jnp.arange(HEADS, dtype=jnp.int32) == line_rank).astype(f32)
    table_grad = jnp.stack([table_sums(tile_one), table_sums(tile_three)])
    table_grad = (own_head[None, :, None] * table_grad[:, None, :]).reshape(128, 3)
    gain_grad = jnp.stack([gain_one, gain_two, gain_three, gain_four])
    gain_grad = gain_grad.reshape(4, 128, 6).transpose(1, 0, 2).reshape(128, 24)
    tiny = jnp.concatenate([gain_grad, grad_router.reshape(128, 48), table_grad], axis=1)
    tiny = jnp.pad(tiny, ((0, 0), (0, 128 - 75))).reshape(4, 2, SLOTS, 128)
    tiny_mine = lax.dynamic_index_in_dim(tiny, core, axis=1, keepdims=False)
    tiny_theirs = lax.dynamic_index_in_dim(tiny, 1 - core, axis=1, keepdims=False)
    tiny_sum = tiny_mine + other_core(tiny_theirs)
    tiny_sum = jnp.pad(tiny_sum.reshape(64, 1, 128), ((0, 0), (0, 5), (0, WIDTH - 128)))
    late_blocks = exchange(jnp.concatenate(late + [tiny_sum.astype(bf16)], axis=1), ("z", "y", "x"))
    late_sum = jnp.sum(late_blocks.astype(f32), axis=0)
    tiny = late_sum[18, :75]

    early_rows = early_sum[:216].reshape(9, 4, 6, WIDTH).transpose(1, 0, 2, 3).reshape(4, 54, WIDTH)
    ffn_out_rows = early_sum[224:320].reshape(3, 4, 8, WIDTH).transpose(1, 0, 2, 3).reshape(4, 24, WIDTH)
    last = jnp.concatenate([ffn_out_rows, early_rows], axis=1)
    last = exchange(jnp.pad(last, ((0, 0), (0, 2), (0, 0))), ("z",))
    last = jnp.sum(last.astype(f32), axis=0)
    six = last[24:78].reshape(9, 6, WIDTH)
    ffn_in_part = six[4:8].transpose(1, 0, 2).reshape(6, 3, 128, 8).transpose(0, 2, 1, 3)
    out_shape = hidden_in.shape
    return (
        hidden_out.reshape(out_shape),
        grad_zero.reshape(out_shape),
        tiny[:24].reshape(4, 6),
        jnp.stack([late_sum[:18].reshape(3, 6, WIDTH), six[0:3]]),
        jnp.stack([six[8], six[3]]),
        tiny[72:75],
        ffn_in_part.reshape(6, FF),
        last[:24],
        tiny[24:72].reshape(6, EXPERTS),
        expert_sum[:192].astype(f32).reshape(4, 48, WIDTH).transpose(1, 0, 2).reshape(1, 48, FF),
        expert_sum[192:].astype(f32).reshape(1, 192, WIDTH),
    )


def solution(mesh):
    fine = Mesh(mesh.devices.reshape(4, 2, 4, 4), ALL)
    return jax.shard_map(
        on_device,
        mesh=fine,
        in_specs=(
            P(None, ALL, None),
            P(None, ROW, None),
            P(None, ALL, None),
            P(None, ALL),
            P(None, None, ALL, None),
            P(None, ALL, None),
            P(ALL),
            P(ALL, None),
            P(ALL, None),
            P(ALL, None),
            P(ROW, LINE, None),
            P(ROW, LINE, None),
            P(None, ALL, None),
        ),
        out_specs=(
            P(None, ALL, None),
            P(None, ALL, None),
            P(None, ALL),
            P(None, None, ALL, None),
            P(None, ALL, None),
            P(ALL),
            P(ALL, None),
            P(ALL, None),
            P(ALL, None),
            P(ROW, LINE, None),
            P(ROW, LINE, None),
        ),
        check_vma=False,
    )
```

```python
import jax
import jax.numpy as jnp
from jax import lax
from jax.experimental import pallas as pl
from jax.experimental.pallas import tpu as pltpu
from jax.sharding import Mesh
from jax.sharding import PartitionSpec as P

WIDTH = 768
HEADS = 12
HEAD_DIM = 64
BUCKETS = 16
EXPERTS = 8
MICRO = 2
TOK = 72
ROWS = MICRO * TOK
GROUP = 1152
CAP = 20
FF = 3072
BLOCK = 128
SLOTS = 16
EPSILON = 1e-06
NEGATIVE = -1e30
SCALE = HEAD_DIM ** (-0.5)
LINE = ("y", "x")
ROW = ("z", "c")
ALL = ("z", "c", "y", "x")

bf16 = jnp.bfloat16
f32 = jnp.float32


def dot(a, b):
    return lax.dot_general(a, b, (((1,), (0,)), ((), ())), preferred_element_type=f32)


def dot_back(a, b):
    return lax.dot_general(a, b, (((1,), (1,)), ((), ())), preferred_element_type=f32)


def dot_outer(a, b):
    return lax.dot_general(a, b, (((0,), (0,)), ((), ())), preferred_element_type=f32)


def normalize(x, scales):
    inv = lax.rsqrt(jnp.mean(x * x, axis=-1, keepdims=True) + EPSILON)
    return (x * inv * scales).astype(bf16), inv


def normalize_back(grad, x, inv, scales):
    scaled = grad * scales
    mean = jnp.mean(scaled * x, axis=-1, keepdims=True)
    grad_x = inv * scaled - x * (inv * inv * inv) * mean
    grad_scales = jnp.sum(grad * x * inv, axis=0)
    return grad_x, grad_scales


def gelu_pair(u):
    root = 0.7978845608028654
    squared = u * u
    t = jnp.tanh(root * u * (1.0 + 0.044715 * squared))
    half = 0.5 * (1.0 + t)
    return u * half, half + 0.5 * u * (1.0 - t * t) * root * (1.0 + 3 * 0.044715 * squared)


def gelu(u):
    return jax.nn.gelu(u, approximate=True)


LIMIT = pltpu.CompilerParams(vmem_limit_bytes=48 * 1024 * 1024)


def split_blocks(blocks_ref, targets):
    whole = blocks_ref[...].astype(f32)
    for j, target in enumerate(targets):
        target[...] = whole[:, j * TOK : (j + 1) * TOK].reshape(GROUP, 2 * HEAD_DIM).astype(bf16)


def forward_kernel(blocks_ref, bias_ref, start_ref, o_ref, lse_ref, qk0_ref, qk1_ref, v_ref):
    split_blocks(blocks_ref, (qk0_ref, qk1_ref, v_ref))
    for m, qk_ref in enumerate((qk0_ref, qk1_ref)):
        lanes = slice(m * HEAD_DIM, (m + 1) * HEAD_DIM)
        keys = qk_ref[:, HEAD_DIM:]
        values = v_ref[:, lanes]
        for i in range(GROUP // BLOCK):
            rows = slice(i * BLOCK, (i + 1) * BLOCK)
            width = (i + 1) * BLOCK
            scores = dot_back(qk_ref[rows, :HEAD_DIM], keys[:width])
            scores = scores + bias_ref[:, GROUP - width :]
            column = lax.broadcasted_iota(jnp.int32, (BLOCK, width), 1)
            scores = jnp.where(column >= start_ref[rows, m : m + 1], scores, NEGATIVE)
            peak = jnp.max(scores, axis=-1, keepdims=True)
            weights = jnp.exp(scores - peak)
            total = jnp.sum(weights, axis=-1, keepdims=True)
            probs = (weights * (1.0 / total)).astype(bf16)
            o_ref[rows, lanes] = dot(probs, values[:width]).astype(bf16)
            lse_ref[rows, m : m + 1] = peak + jnp.log(total)


def backward_kernel(
    blocks_ref, do_ref, bias_ref, start_ref, lse_ref, grads_ref, table_ref,
    qk0_ref, qk1_ref, v_ref, dqk0_ref, dqk1_ref, dv_ref, dk_acc, dv_acc,
):
    split_blocks(blocks_ref, (qk0_ref, qk1_ref, v_ref))
    table_ref[...] = jnp.zeros_like(table_ref)
    for m, (qk_ref, dqk_ref) in enumerate(((qk0_ref, dqk0_ref), (qk1_ref, dqk1_ref))):
        lanes = slice(m * HEAD_DIM, (m + 1) * HEAD_DIM)
        keys = qk_ref[:, HEAD_DIM:]
        values = v_ref[:, lanes]
        dk_acc[...] = jnp.zeros_like(dk_acc)
        dv_acc[...] = jnp.zeros_like(dv_acc)
        for i in range(GROUP // BLOCK):
            rows = slice(i * BLOCK, (i + 1) * BLOCK)
            width = (i + 1) * BLOCK
            query = qk_ref[rows, :HEAD_DIM]
            grad_o = do_ref[rows, lanes]
            scores = dot_back(query, keys[:width]) + bias_ref[:, GROUP - width :]
            column = lax.broadcasted_iota(jnp.int32, (BLOCK, width), 1)
            scores = jnp.where(column >= start_ref[rows, m : m + 1], scores, NEGATIVE)
            probs = jnp.exp(scores - lse_ref[rows, m : m + 1])
            grad_probs = dot_back(grad_o, values[:width])
            weighted = probs * grad_probs
            inner = jnp.sum(weighted, axis=-1, keepdims=True)
            grad_scores = (weighted - probs * inner).astype(bf16)
            table_ref[:, GROUP - width :] += grad_scores.astype(f32)
            dqk_ref[rows, :HEAD_DIM] = dot(grad_scores, keys[:width]) * SCALE
            dk_acc[:width] += dot_outer(grad_scores, query)
            dv_acc[:width] += dot_outer(probs.astype(bf16), grad_o)
        dqk_ref[:, HEAD_DIM:] = dk_acc[...]
        dv_ref[:, lanes] = dv_acc[...]
    parts = [r[...].reshape(SLOTS, TOK, 2 * HEAD_DIM) for r in (dqk0_ref, dqk1_ref, dv_ref)]
    grads_ref[...] = jnp.concatenate(parts, axis=1).astype(bf16)


def swap(values):
    return pltpu.roll(values, HEAD_DIM, 1)


def low_half(rows):
    return lax.broadcasted_iota(jnp.int32, (rows, 2 * HEAD_DIM), 1) < HEAD_DIM


def interleave(first, second):
    low = low_half(first.shape[0])
    return jnp.where(low, first, swap(second)), jnp.where(low, swap(first), second)


def pair_lanes(pair, offset=0):
    return slice(offset + pair * 2 * HEAD_DIM, offset + (pair + 1) * 2 * HEAD_DIM)


def pack_qkv_kernel(qkv_ref, out_ref):
    for pair in range(HEADS // 2):
        q = qkv_ref[:, pair_lanes(pair)] * SCALE
        k = qkv_ref[:, pair_lanes(pair, WIDTH)]
        v = qkv_ref[:, pair_lanes(pair, 2 * WIDTH)]
        heads = interleave(q, k)
        values = interleave(v[:TOK], v[TOK:])
        for j in range(2):
            out_ref[2 * pair + j] = jnp.concatenate([heads[j], values[j]], axis=0).astype(bf16)
    for slot in range(HEADS, SLOTS):
        out_ref[slot] = jnp.zeros_like(out_ref[slot])


def unpack_qkv_kernel(in_ref, out_ref):
    for pair in range(HEADS // 2):
        even, odd = in_ref[2 * pair].astype(f32), in_ref[2 * pair + 1].astype(f32)
        q, k = interleave(even[:ROWS], odd[:ROWS])
        v = jnp.concatenate(interleave(even[ROWS:], odd[ROWS:]), axis=0)
        for j, value in enumerate((q, k, v)):
            out_ref[:, pair_lanes(pair, j * WIDTH)] = value.astype(bf16)


def pack_one_kernel(in_ref, out_ref):
    for pair in range(HEADS // 2):
        values = in_ref[:, pair_lanes(pair)]
        for j, value in enumerate(interleave(values[:TOK], values[TOK:])):
            out_ref[2 * pair + j] = value.astype(bf16)
    for slot in range(HEADS, SLOTS):
        out_ref[slot] = jnp.zeros_like(out_ref[slot])


def unpack_one_kernel(in_ref, out_ref):
    for pair in range(HEADS // 2):
        even, odd = in_ref[2 * pair].astype(f32), in_ref[2 * pair + 1].astype(f32)
        values = jnp.concatenate(interleave(even, odd), axis=0)
        out_ref[:, pair_lanes(pair)] = values.astype(bf16)


def repack(kernel, shape, values):
    return pl.pallas_call(
        kernel,
        out_shape=jax.ShapeDtypeStruct(shape, bf16),
        compiler_params=LIMIT,
        cost_estimate=pl.CostEstimate(flops=1000000, bytes_accessed=1500000, transcendentals=0),
    )(values)


LINE_ROWS = 704
EXPERT_ROWS = 384
STEP = 256


def rows_of(a, b, count):
    return dot_outer(a[...], b[...]).reshape(SLOTS, count, -1)


def put(out_ref, first, parts):
    value = jnp.concatenate(parts, axis=1).astype(bf16)
    out_ref[:, first : first + value.shape[1]] = value


def expert_products_kernel(a_rows, b_due0, b_due1, b_due2, b_due3, a_hidden, b_rows, out_ref):
    put(out_ref, 0, [rows_of(a_rows, b, 48) for b in (b_due0, b_due1, b_due2, b_due3)])
    put(out_ref, 192, [rows_of(a_hidden, b_rows, 192)])


def shared_products_kernel(
    a_qkv, b_q, b_k, b_v, a_out, b_out, a_in, b_in0, b_in1, b_in2, b_in3, a_zero, b_zero, a_second, b_second,
    buffer_ref, out_ref, staged,
):
    block = pl.program_id(1)

    @pl.when(block == 0)
    def _():
        put(staged, 0, [rows_of(a_qkv, b, 24) for b in (b_q, b_k, b_v)] + [rows_of(a_out, b_out, 24)])
        put(staged, 96, [rows_of(a_in, b, 24) for b in (b_in0, b_in1, b_in2, b_in3)])
        zero = rows_of(a_zero, b_zero, 24)
        put(staged, 192, [zero, jnp.zeros_like(zero[:, :8])])
        second = dot_outer(a_second[...], b_second[...]).reshape(12, SLOTS, 8, -1)
        put(staged, 224, [second[j] for j in range(12)])

    out_ref[...] = staged[:, pl.ds(pl.multiple_of(block * 64, 64), 64), :]


def product_operands(pairs, counts):
    operands, specs, flops = [], [], 0
    for (a, b), count in zip(pairs, counts):
        operands.append(a)
        specs.append(pl.BlockSpec(a.shape, lambda n, *rest: (0, 0)))
        flops += 2 * a.size * b.shape[1]
        for j in range(count):
            operands.append(b)
            specs.append(
                pl.BlockSpec((b.shape[0], STEP), lambda n, *rest, j=j: (0, n + j * (WIDTH // STEP)))
            )
    return operands, specs, flops


def expert_products(expert_in, expert_out):
    operands, specs, flops = product_operands((expert_in, expert_out), (4, 1))
    return pl.pallas_call(
        expert_products_kernel,
        grid=(WIDTH // STEP,),
        in_specs=specs,
        out_specs=pl.BlockSpec((SLOTS, EXPERT_ROWS, STEP), lambda n: (0, 0, n)),
        out_shape=jax.ShapeDtypeStruct((SLOTS, LINE_ROWS, WIDTH), bf16),
        compiler_params=LIMIT,
        cost_estimate=pl.CostEstimate(flops=flops, bytes_accessed=15000000, transcendentals=0),
    )(*operands)


def shared_products(pairs, buffer):
    operands, specs, flops = product_operands(pairs, (3, 1, 4, 1, 1))
    return pl.pallas_call(
        shared_products_kernel,
        grid=(WIDTH // STEP, (LINE_ROWS - EXPERT_ROWS) // 64),
        in_specs=specs + [pl.BlockSpec(memory_space=pl.ANY)],
        out_specs=pl.BlockSpec((SLOTS, 64, STEP), lambda n, r: (0, EXPERT_ROWS // 64 + r, n)),
        out_shape=jax.ShapeDtypeStruct((SLOTS, LINE_ROWS, WIDTH), bf16),
        scratch_shapes=[pltpu.VMEM((SLOTS, LINE_ROWS - EXPERT_ROWS, STEP), bf16)],
        input_output_aliases={len(operands): 0},
        compiler_params=LIMIT,
        cost_estimate=pl.CostEstimate(flops=flops, bytes_accessed=15000000, transcendentals=0),
    )(*operands, buffer)


def expert_kernel(
    arrived_ref, w_in_ref, w_out_ref, produced_ref, rows_ref, grads_ref, hidden_ref, due_ref, forward_acc, back_acc
):
    step = pl.program_id(0)

    @pl.when(step == 0)
    def _():
        whole = arrived_ref[...].astype(f32)
        rows_ref[...] = whole[:, :40].reshape(320, WIDTH).astype(bf16)
        grads_ref[...] = whole[:, 40:].reshape(320, WIDTH).astype(bf16)
        forward_acc[...] = jnp.zeros_like(forward_acc)
        back_acc[...] = jnp.zeros_like(back_acc)

    u = dot(rows_ref[...], w_in_ref[...])
    grad_hidden = dot_back(grads_ref[...], w_out_ref[...])
    hidden, slope = gelu_pair(u)
    hidden = hidden.astype(bf16)
    due = (grad_hidden * slope).astype(bf16)
    hidden_ref[...] = hidden
    due_ref[...] = due
    forward_acc[...] += dot(hidden, w_out_ref[...])
    back_acc[...] += dot_back(due, w_in_ref[...])

    @pl.when(step == pl.num_programs(0) - 1)
    def _():
        parts = [a[...].reshape(EXPERTS, 40, WIDTH) for a in (forward_acc, back_acc)]
        produced_ref[...] = jnp.concatenate(parts, axis=1).astype(bf16)


def expert_block(arrived, w_in, w_out):
    def fixed(shape):
        return pl.BlockSpec(shape, lambda n: (0,) * len(shape))

    rows = jax.ShapeDtypeStruct((320, WIDTH), bf16)
    units = jax.ShapeDtypeStruct((320, FF), bf16)
    return pl.pallas_call(
        expert_kernel,
        grid=(FF // 512,),
        in_specs=[
            fixed((EXPERTS, 80, WIDTH)),
            pl.BlockSpec((WIDTH, 512), lambda n: (0, n)),
            pl.BlockSpec((512, WIDTH), lambda n: (n, 0)),
        ],
        out_specs=(
            fixed((EXPERTS, 80, WIDTH)),
            fixed((320, WIDTH)),
            fixed((320, WIDTH)),
            pl.BlockSpec((320, 512), lambda n: (0, n)),
            pl.BlockSpec((320, 512), lambda n: (0, n)),
        ),
        out_shape=(jax.ShapeDtypeStruct((EXPERTS, 80, WIDTH), bf16), rows, rows, units, units),
        scratch_shapes=[pltpu.VMEM((320, WIDTH), f32), pltpu.VMEM((320, WIDTH), f32)],
        compiler_params=LIMIT,
        cost_estimate=pl.CostEstimate(
            flops=8 * 320 * WIDTH * FF, bytes_accessed=15000000, transcendentals=320 * FF
        ),
    )(arrived, w_in, w_out)


def staging(dtype, count):
    return [pltpu.VMEM((GROUP, 2 * HEAD_DIM), dtype)] * count


def head_forward(blocks, bias, start):
    return pl.pallas_call(
        forward_kernel,
        out_shape=(
            jax.ShapeDtypeStruct((GROUP, 2 * HEAD_DIM), bf16),
            jax.ShapeDtypeStruct((GROUP, MICRO), f32),
        ),
        scratch_shapes=staging(bf16, 3),
        compiler_params=LIMIT,
        cost_estimate=pl.CostEstimate(
            flops=4 * MICRO * GROUP * GROUP * HEAD_DIM // 2,
            bytes_accessed=6 * GROUP * 256,
            transcendentals=MICRO * GROUP * GROUP // 2,
        ),
    )(blocks, bias, start)


def head_backward(blocks, grad_o, bias, start, lse):
    return pl.pallas_call(
        backward_kernel,
        out_shape=(
            jax.ShapeDtypeStruct((SLOTS, 3 * TOK, 2 * HEAD_DIM), bf16),
            jax.ShapeDtypeStruct((BLOCK, GROUP), f32),
        ),
        scratch_shapes=staging(bf16, 3)
        + staging(f32, 3)
        + [pltpu.VMEM((GROUP, HEAD_DIM), f32), pltpu.VMEM((GROUP, HEAD_DIM), f32)],
        compiler_params=LIMIT,
        cost_estimate=pl.CostEstimate(
            flops=10 * MICRO * GROUP * GROUP * HEAD_DIM // 2,
            bytes_accessed=12 * GROUP * 256,
            transcendentals=MICRO * GROUP * GROUP // 2,
        ),
    )(blocks, grad_o, bias, start, lse)


def tile_distance():
    row = lax.broadcasted_iota(jnp.int32, (BLOCK, GROUP), 0)
    column = lax.broadcasted_iota(jnp.int32, (BLOCK, GROUP), 1)
    return row - column + (GROUP - BLOCK)


def bucket_starts():
    return [0, 1, 2, 3, 4, 5, 6, 7] + [2**t for t in range(3, 11)]


def bias_tile(entries):
    distance = tile_distance()
    result = jnp.full((BLOCK, GROUP), NEGATIVE, f32)
    for b, first in enumerate(bucket_starts()):
        result = jnp.where(distance >= first, entries[b], result)
    return result


def table_sums(tile):
    distance = tile_distance()
    first = jnp.array(bucket_starts(), jnp.int32)[:, None, None]
    last = jnp.array(bucket_starts()[1:] + [GROUP], jnp.int32)[:, None, None]
    inside = (distance[None] >= first) & (distance[None] < last)
    return jnp.sum(jnp.where(inside, tile[None], 0.0), axis=(1, 2))


def exchange(blocks, axes):
    return lax.all_to_all(blocks, axes, split_axis=0, concat_axis=0, tiled=True)


def spread_matrix():
    out = lax.broadcasted_iota(jnp.int32, (WIDTH, 1024), 1)
    source = lax.broadcasted_iota(jnp.int32, (WIDTH, 1024), 0)
    return ((out % 8 < 6) & (source == out // 8 * 6 + out % 8)).astype(bf16)


def spread(values, places):
    return dot(values, places).astype(bf16)


def gather_back(values, places):
    return dot_back(values.astype(bf16), places)


HEAD_SHAPE = (SLOTS, 3 * TOK, 2 * HEAD_DIM)
ONE_SHAPE = (SLOTS, TOK, 2 * HEAD_DIM)


def attend_forward(x, scales, w_qkv, w_out, places, bias, start):
    normed, inv = normalize(x, scales)
    blocks = exchange(repack(pack_qkv_kernel, HEAD_SHAPE, dot(spread(normed, places), w_qkv)), LINE)
    o, lse = head_forward(blocks, bias, start)
    attended = repack(unpack_one_kernel, (ROWS, WIDTH), exchange(o.reshape(ONE_SHAPE), LINE))
    x = x + dot(spread(attended, places), w_out)
    return x, (normed, inv, blocks, lse, attended)


def attend_backward(grad, x, scales, w_qkv, w_out, places, bias, start, saved):
    normed, inv, blocks, lse, attended = saved
    branch = grad.astype(bf16)
    grad_attended = gather_back(dot_back(branch, w_out), places)
    grad_o = exchange(repack(pack_one_kernel, ONE_SHAPE, grad_attended), LINE)
    grad_heads, tile = head_backward(blocks, grad_o.reshape(GROUP, 2 * HEAD_DIM), bias, start, lse)
    heads = repack(unpack_qkv_kernel, (ROWS, 3 * WIDTH), exchange(grad_heads, LINE))
    grad_normed = gather_back(dot_back(heads, w_qkv), places)
    grad_x, grad_scales = normalize_back(grad_normed, x, inv, scales)
    return grad + grad_x, grad_scales, branch, heads, tile


def other_core(value):
    return lax.ppermute(value, "c", [(0, 1), (1, 0)])


def select_columns(core, line_first):
    out = lax.broadcasted_iota(jnp.int32, (WIDTH, WIDTH // 2), 1)
    source = lax.broadcasted_iota(jnp.int32, (WIDTH, WIDTH // 2), 0)
    outer, i = out // 6, out % 6
    z, line = (outer % 4, outer // 4) if line_first else (outer // SLOTS, outer % SLOTS)
    return (source == ((z * 2 + core) * SLOTS + line) * 6 + i).astype(bf16)


def pick(a, selector):
    return dot(a, selector).astype(bf16)


def on_device(
    hidden_in, lengths, routes, norm_gains, qkv_weights, out_weights, rel_table,
    ffn_in, ffn_out, router, expert_in, expert_out, cotangent,
):
    core = lax.axis_index("c")
    line_rank = lax.axis_index("y") * 4 + lax.axis_index("x")

    places = spread_matrix()
    ffn_in_units = ffn_in.reshape(6, 128, 3, 8).transpose(0, 2, 1, 3).reshape(6, FF)
    attention = [
        jnp.concatenate([qkv_weights[l, 0], qkv_weights[l, 1], qkv_weights[l, 2], out_weights[l]], axis=1)
        for l in range(2)
    ]
    pack = jnp.pad(jnp.concatenate(attention + [ffn_in_units], axis=1), ((0, 2), (0, 0)))
    pack = jnp.concatenate([pack, ffn_out[:8], ffn_out[8:16], ffn_out[16:]], axis=1)
    shared = lax.all_gather(pack, ALL, axis=0, tiled=True)
    w_expert_in = lax.all_gather(expert_in[0], LINE, axis=0, tiled=True)
    w_expert_out = lax.all_gather(expert_out[0], LINE, axis=0, tiled=True)
    qkv_zero, out_zero = shared[:, : 3 * WIDTH], shared[:, 3 * WIDTH : 4 * WIDTH]
    qkv_one, out_one = shared[:, 4 * WIDTH : 7 * WIDTH], shared[:, 7 * WIDTH : 8 * WIDTH]
    w_in = shared[:, 8 * WIDTH : 12 * WIDTH]
    w_out = [shared[:, (12 + g) * WIDTH : (13 + g) * WIDTH] for g in range(3)]

    small = jnp.concatenate([norm_gains.reshape(24), router.reshape(48), rel_table])
    small = jnp.pad(small, (0, 128 - 75))[None, None, :]
    small = jnp.broadcast_to(small, (SLOTS, 8, 128))
    small = exchange(small, LINE).reshape(1, 128, 128)
    small = exchange(jnp.broadcast_to(small, (EXPERTS, 128, 128)), ROW)
    small = small.reshape(128, 8, 128)[:, 0]
    gains = small[:, :24].reshape(128, 4, 6).transpose(1, 0, 2).reshape(4, WIDTH).astype(f32)
    w_router = small[:, 24:72].reshape(WIDTH, EXPERTS)
    table = small[:, 72:75].reshape(2, HEADS, BUCKETS).astype(f32)
    head = jnp.minimum(line_rank, HEADS - 1)
    entries = lax.dynamic_index_in_dim(table, head, axis=1, keepdims=False)
    bias = [bias_tile(entries[layer]) for layer in range(2)]

    ends = jnp.cumsum(lengths[:, 0], axis=1)
    position = jnp.arange(GROUP, dtype=jnp.int32)[:, None, None]
    start = jnp.max(jnp.where(position >= ends[None], ends[None], 0), axis=2)

    x0 = hidden_in.reshape(ROWS, WIDTH).astype(f32)
    x1, saved_one = attend_forward(x0, gains[0], qkv_zero, out_zero, places, bias[0], start)
    c, inv_c = normalize(x1, gains[1])
    u = dot(spread(c, places), w_in)
    h = gelu(u).astype(bf16)
    x2 = x1 + sum(dot(h[:, g * 1024 : (g + 1) * 1024], w_out[g]) for g in range(3))
    x3, saved_three = attend_forward(x2, gains[2], qkv_one, out_one, places, bias[1], start)

    e, inv_e = normalize(x3, gains[3])
    logits = dot(e, w_router)
    choice = routes.reshape(ROWS, 2)
    marks = (choice[:, :, None] == jnp.arange(EXPERTS, dtype=jnp.int32)).astype(f32)
    chosen = jnp.sum(marks * logits[:, None, :], axis=-1)
    gates = jax.nn.softmax(chosen, axis=-1)
    pair_marks = marks.reshape(MICRO, TOK * 2, EXPERTS)
    earlier = jnp.cumsum(pair_marks, axis=1) - pair_marks
    slots = jnp.sum(earlier * pair_marks, axis=-1).astype(jnp.int32).reshape(ROWS, 2)
    micro = (jnp.arange(ROWS, dtype=jnp.int32) // TOK)[:, None]
    target = choice * 80 + micro * CAP + slots
    target_k = target.T
    row_id = jnp.arange(EXPERTS * 80, dtype=jnp.int32)
    place = [row_id[:, None] == target_k[k][None, :] for k in range(2)]
    place_back = [row_id[:, None] == target_k[k][None, :] + 40 for k in range(2)]
    scatter = jnp.concatenate([place[0] | place[1], place_back[0], place_back[1]], axis=1).astype(bf16)
    collect = jnp.concatenate([place_back[0] | place_back[1], place[0], place[1]], axis=1).astype(bf16)
    grad_four = cotangent.reshape(ROWS, WIDTH).astype(f32)
    picked_grads = [(gates[:, k : k + 1] * grad_four).astype(bf16) for k in range(2)]
    sent = dot(scatter, jnp.concatenate([e] + picked_grads, axis=0)).astype(bf16)
    arrived = exchange(sent.reshape(EXPERTS, 80, WIDTH), ROW)
    produced, expert_rows, grad_rows, he, due = expert_block(arrived, w_expert_in, w_expert_out)
    buffer = expert_products((expert_rows, due), (he, grad_rows))
    returned = exchange(produced, ROW).reshape(EXPERTS * 80, WIDTH)
    collected = dot_outer(collect, returned)
    picked = [collected[ROWS : 2 * ROWS], collected[2 * ROWS :]]
    hidden_out = x3 + gates[:, :1] * picked[0] + gates[:, 1:] * picked[1]

    dgates = jnp.stack([jnp.sum(grad_four * p, axis=-1) for p in picked], axis=1)
    dchosen = gates * (dgates - jnp.sum(gates * dgates, axis=-1, keepdims=True))
    dlogits = jnp.sum(marks * dchosen[:, :, None], axis=1)
    grad_router = dot_outer(e, dlogits.astype(bf16))
    grad_e = collected[:ROWS] + dot_back(dlogits.astype(bf16), w_router)
    grad_x, gain_four = normalize_back(grad_e, x3, inv_e, gains[3])
    grad_three = grad_four + grad_x + 0.0 * buffer[0, 0, 0].astype(f32)


    def share(a, b, line_first):
        mine = pick(a, select_columns(core, line_first))
        theirs = pick(a, select_columns(1 - core, line_first))
        got = other_core(jnp.concatenate([theirs, b], axis=1))
        return (
            jnp.concatenate([mine, got[:, : WIDTH // 2]], axis=0),
            jnp.concatenate([b, got[:, WIDTH // 2 :]], axis=0),
        )

    def chunks(a, b, count):
        return [
            dot_outer(a, b[:, j * WIDTH : (j + 1) * WIDTH]).astype(bf16).reshape(count, -1, WIDTH)
            for j in range(b.shape[1] // WIDTH)
        ]

    grad_two, gain_three, branch_three, heads_three, tile_three = attend_backward(
        grad_three, x2, gains[2], qkv_one, out_one, places, bias[1], start, saved_three
    )
    pair_qkv = share(saved_three[0], heads_three, True)
    pair_out = share(saved_three[4], branch_three, True)

    branch_two = grad_two.astype(bf16)
    grad_h = jnp.concatenate([dot_back(branch_two, w) for w in w_out], axis=1)
    gelu_back_two = jax.vjp(gelu, u)[1]
    du = gelu_back_two(grad_h)[0].astype(bf16)
    grad_c = gather_back(dot_back(du, w_in), places)
    grad_x, gain_two = normalize_back(grad_c, x1, inv_c, gains[1])
    grad_one = grad_two + grad_x
    pair_in = share(c, du, True)
    pair_zero = share(saved_one[4], grad_one.astype(bf16), True)
    halves = h.reshape(ROWS, 12, 2, BLOCK)
    mine = lax.dynamic_index_in_dim(halves, core, axis=2, keepdims=False).reshape(ROWS, FF // 2)
    theirs = lax.dynamic_index_in_dim(halves, 1 - core, axis=2, keepdims=False).reshape(ROWS, FF // 2)
    got = other_core(jnp.concatenate([theirs, branch_two], axis=1))
    mine = jnp.concatenate([mine, got[:, : FF // 2]], axis=0)
    pair_second = (mine, jnp.concatenate([branch_two, got[:, FF // 2 :]], axis=0))
    summed = shared_products((pair_qkv, pair_out, pair_in, pair_zero, pair_second), buffer)
    early_sum = lax.optimization_barrier(
        lax.psum_scatter(summed, LINE, scatter_dimension=0, tiled=False)
    )
    expert_sum, early_sum = early_sum[:EXPERT_ROWS], early_sum[EXPERT_ROWS:]

    grad_zero, gain_one, branch_one, heads_one, tile_one = attend_backward(
        grad_one, x0, gains[0], qkv_zero, out_zero, places, bias[0], start, saved_one
    )
    late = chunks(*share(saved_one[0], heads_one, False), 64)

    own_head = (jnp.arange(HEADS, dtype=jnp.int32) == line_rank).astype(f32)
    table_grad = jnp.stack([table_sums(tile_one), table_sums(tile_three)])
    table_grad = (own_head[None, :, None] * table_grad[:, None, :]).reshape(128, 3)
    gain_grad = jnp.stack([gain_one, gain_two, gain_three, gain_four])
    gain_grad = gain_grad.reshape(4, 128, 6).transpose(1, 0, 2).reshape(128, 24)
    tiny = jnp.concatenate([gain_grad, grad_router.reshape(128, 48), table_grad], axis=1)
    tiny = jnp.pad(tiny, ((0, 0), (0, 128 - 75))).reshape(4, 2, SLOTS, 128)
    tiny_mine = lax.dynamic_index_in_dim(tiny, core, axis=1, keepdims=False)
    tiny_theirs = lax.dynamic_index_in_dim(tiny, 1 - core, axis=1, keepdims=False)
    tiny_sum = tiny_mine + other_core(tiny_theirs)
    tiny_sum = jnp.pad(tiny_sum.reshape(64, 1, 128), ((0, 0), (0, 5), (0, WIDTH - 128)))
    late_blocks = exchange(jnp.concatenate(late + [tiny_sum.astype(bf16)], axis=1), ("z", "y", "x"))
    late_sum = jnp.sum(late_blocks.astype(f32), axis=0)
    tiny = late_sum[18, :75]

    early_rows = early_sum[:216].reshape(9, 4, 6, WIDTH).transpose(1, 0, 2, 3).reshape(4, 54, WIDTH)
    ffn_out_rows = early_sum[224:320].reshape(3, 4, 8, WIDTH).transpose(1, 0, 2, 3).reshape(4, 24, WIDTH)
    last = jnp.concatenate([ffn_out_rows, early_rows], axis=1)
    last = exchange(jnp.pad(last, ((0, 0), (0, 2), (0, 0))), ("z",))
    last = jnp.sum(last.astype(f32), axis=0)
    six = last[24:78].reshape(9, 6, WIDTH)
    ffn_in_part = six[4:8].transpose(1, 0, 2).reshape(6, 3, 128, 8).transpose(0, 2, 1, 3)
    out_shape = hidden_in.shape
    return (
        hidden_out.reshape(out_shape),
        grad_zero.reshape(out_shape),
        tiny[:24].reshape(4, 6),
        jnp.stack([late_sum[:18].reshape(3, 6, WIDTH), six[0:3]]),
        jnp.stack([six[8], six[3]]),
        tiny[72:75],
        ffn_in_part.reshape(6, FF),
        last[:24],
        tiny[24:72].reshape(6, EXPERTS),
        expert_sum[:192].astype(f32).reshape(4, 48, WIDTH).transpose(1, 0, 2).reshape(1, 48, FF),
        expert_sum[192:].astype(f32).reshape(1, 192, WIDTH),
    )


def solution(mesh):
    fine = Mesh(mesh.devices.reshape(4, 2, 4, 4), ALL)
    return jax.shard_map(
        on_device,
        mesh=fine,
        in_specs=(
            P(None, ALL, None),
            P(None, ROW, None),
            P(None, ALL, None),
            P(None, ALL),
            P(None, None, ALL, None),
            P(None, ALL, None),
            P(ALL),
            P(ALL, None),
            P(ALL, None),
            P(ALL, None),
            P(ROW, LINE, None),
            P(ROW, LINE, None),
            P(None, ALL, None),
        ),
        out_specs=(
            P(None, ALL, None),
            P(None, ALL, None),
            P(None, ALL),
            P(None, None, ALL, None),
            P(None, ALL, None),
            P(ALL),
            P(ALL, None),
            P(ALL, None),
            P(ALL, None),
            P(ROW, LINE, None),
            P(ROW, LINE, None),
        ),
        check_vma=False,
    )
```

```python
import jax
import jax.numpy as jnp
from jax import lax
from jax.experimental import pallas as pl
from jax.experimental.pallas import tpu as pltpu
from jax.sharding import Mesh
from jax.sharding import PartitionSpec as P

WIDTH = 768
HEADS = 12
HEAD_DIM = 64
BUCKETS = 16
EXPERTS = 8
MICRO = 2
TOK = 72
ROWS = MICRO * TOK
GROUP = 1152
CAP = 20
FF = 3072
BLOCK = 128
SLOTS = 16
EPSILON = 1e-06
NEGATIVE = -1e30
SCALE = HEAD_DIM ** (-0.5)
LINE = ("y", "x")
ROW = ("z", "c")
ALL = ("z", "c", "y", "x")

bf16 = jnp.bfloat16
f32 = jnp.float32


def dot(a, b):
    return lax.dot_general(a, b, (((1,), (0,)), ((), ())), preferred_element_type=f32)


def dot_back(a, b):
    return lax.dot_general(a, b, (((1,), (1,)), ((), ())), preferred_element_type=f32)


def dot_outer(a, b):
    return lax.dot_general(a, b, (((0,), (0,)), ((), ())), preferred_element_type=f32)


def normalize(x, scales):
    inv = lax.rsqrt(jnp.mean(x * x, axis=-1, keepdims=True) + EPSILON)
    return (x * inv * scales).astype(bf16), inv


def normalize_back(grad, x, inv, scales):
    scaled = grad * scales
    mean = jnp.mean(scaled * x, axis=-1, keepdims=True)
    grad_x = inv * scaled - x * (inv * inv * inv) * mean
    grad_scales = jnp.sum(grad * x * inv, axis=0)
    return grad_x, grad_scales


def gelu_pair(u):
    root = 0.7978845608028654
    squared = u * u
    t = jnp.tanh(root * u * (1.0 + 0.044715 * squared))
    half = 0.5 * (1.0 + t)
    return u * half, half + 0.5 * u * (1.0 - t * t) * root * (1.0 + 3 * 0.044715 * squared)


def gelu(u):
    return jax.nn.gelu(u, approximate=True)


LIMIT = pltpu.CompilerParams(vmem_limit_bytes=48 * 1024 * 1024)


def split_blocks(blocks_ref, targets):
    whole = blocks_ref[...].astype(f32)
    for j, target in enumerate(targets):
        target[...] = whole[:, j * TOK : (j + 1) * TOK].reshape(GROUP, 2 * HEAD_DIM).astype(bf16)


def forward_kernel(blocks_ref, bias_ref, start_ref, o_ref, lse_ref, qk0_ref, qk1_ref, v_ref):
    split_blocks(blocks_ref, (qk0_ref, qk1_ref, v_ref))
    for m, qk_ref in enumerate((qk0_ref, qk1_ref)):
        lanes = slice(m * HEAD_DIM, (m + 1) * HEAD_DIM)
        keys = qk_ref[:, HEAD_DIM:]
        values = v_ref[:, lanes]
        for i in range(GROUP // BLOCK):
            rows = slice(i * BLOCK, (i + 1) * BLOCK)
            width = (i + 1) * BLOCK
            scores = dot_back(qk_ref[rows, :HEAD_DIM], keys[:width])
            scores = scores + bias_ref[:, GROUP - width :]
            column = lax.broadcasted_iota(jnp.int32, (BLOCK, width), 1)
            scores = jnp.where(column >= start_ref[rows, m : m + 1], scores, NEGATIVE)
            peak = jnp.max(scores, axis=-1, keepdims=True)
            weights = jnp.exp(scores - peak)
            total = jnp.sum(weights, axis=-1, keepdims=True)
            probs = (weights * (1.0 / total)).astype(bf16)
            o_ref[rows, lanes] = dot(probs, values[:width]).astype(bf16)
            lse_ref[rows, m : m + 1] = peak + jnp.log(total)


def backward_kernel(
    blocks_ref, do_ref, bias_ref, start_ref, lse_ref, grads_ref, table_ref,
    qk0_ref, qk1_ref, v_ref, dqk0_ref, dqk1_ref, dv_ref, dk_acc, dv_acc,
):
    split_blocks(blocks_ref, (qk0_ref, qk1_ref, v_ref))
    table_ref[...] = jnp.zeros_like(table_ref)
    for m, (qk_ref, dqk_ref) in enumerate(((qk0_ref, dqk0_ref), (qk1_ref, dqk1_ref))):
        lanes = slice(m * HEAD_DIM, (m + 1) * HEAD_DIM)
        keys = qk_ref[:, HEAD_DIM:]
        values = v_ref[:, lanes]
        dk_acc[...] = jnp.zeros_like(dk_acc)
        dv_acc[...] = jnp.zeros_like(dv_acc)
        for i in range(GROUP // BLOCK):
            rows = slice(i * BLOCK, (i + 1) * BLOCK)
            width = (i + 1) * BLOCK
            query = qk_ref[rows, :HEAD_DIM]
            grad_o = do_ref[rows, lanes]
            scores = dot_back(query, keys[:width]) + bias_ref[:, GROUP - width :]
            column = lax.broadcasted_iota(jnp.int32, (BLOCK, width), 1)
            scores = jnp.where(column >= start_ref[rows, m : m + 1], scores, NEGATIVE)
            probs = jnp.exp(scores - lse_ref[rows, m : m + 1])
            grad_probs = dot_back(grad_o, values[:width])
            weighted = probs * grad_probs
            inner = jnp.sum(weighted, axis=-1, keepdims=True)
            grad_scores = (weighted - probs * inner).astype(bf16)
            table_ref[:, GROUP - width :] += grad_scores.astype(f32)
            dqk_ref[rows, :HEAD_DIM] = dot(grad_scores, keys[:width]) * SCALE
            dk_acc[:width] += dot_outer(grad_scores, query)
            dv_acc[:width] += dot_outer(probs.astype(bf16), grad_o)
        dqk_ref[:, HEAD_DIM:] = dk_acc[...]
        dv_ref[:, lanes] = dv_acc[...]
    parts = [r[...].reshape(SLOTS, TOK, 2 * HEAD_DIM) for r in (dqk0_ref, dqk1_ref, dv_ref)]
    grads_ref[...] = jnp.concatenate(parts, axis=1).astype(bf16)


def swap(values):
    return pltpu.roll(values, HEAD_DIM, 1)


def low_half(rows):
    return lax.broadcasted_iota(jnp.int32, (rows, 2 * HEAD_DIM), 1) < HEAD_DIM


def interleave(first, second):
    low = low_half(first.shape[0])
    return jnp.where(low, first, swap(second)), jnp.where(low, swap(first), second)


def pair_lanes(pair, offset=0):
    return slice(offset + pair * 2 * HEAD_DIM, offset + (pair + 1) * 2 * HEAD_DIM)


def pack_qkv_kernel(qkv_ref, out_ref):
    for pair in range(HEADS // 2):
        q = qkv_ref[:, pair_lanes(pair)] * SCALE
        k = qkv_ref[:, pair_lanes(pair, WIDTH)]
        v = qkv_ref[:, pair_lanes(pair, 2 * WIDTH)]
        heads = interleave(q, k)
        values = interleave(v[:TOK], v[TOK:])
        for j in range(2):
            out_ref[2 * pair + j] = jnp.concatenate([heads[j], values[j]], axis=0).astype(bf16)
    for slot in range(HEADS, SLOTS):
        out_ref[slot] = jnp.zeros_like(out_ref[slot])


def unpack_qkv_kernel(in_ref, out_ref):
    for pair in range(HEADS // 2):
        even, odd = in_ref[2 * pair].astype(f32), in_ref[2 * pair + 1].astype(f32)
        q, k = interleave(even[:ROWS], odd[:ROWS])
        v = jnp.concatenate(interleave(even[ROWS:], odd[ROWS:]), axis=0)
        for j, value in enumerate((q, k, v)):
            out_ref[:, pair_lanes(pair, j * WIDTH)] = value.astype(bf16)


def pack_one_kernel(in_ref, out_ref):
    for pair in range(HEADS // 2):
        values = in_ref[:, pair_lanes(pair)]
        for j, value in enumerate(interleave(values[:TOK], values[TOK:])):
            out_ref[2 * pair + j] = value.astype(bf16)
    for slot in range(HEADS, SLOTS):
        out_ref[slot] = jnp.zeros_like(out_ref[slot])


def unpack_one_kernel(in_ref, out_ref):
    for pair in range(HEADS // 2):
        even, odd = in_ref[2 * pair].astype(f32), in_ref[2 * pair + 1].astype(f32)
        values = jnp.concatenate(interleave(even, odd), axis=0)
        out_ref[:, pair_lanes(pair)] = values.astype(bf16)


def repack(kernel, shape, values):
    return pl.pallas_call(
        kernel,
        out_shape=jax.ShapeDtypeStruct(shape, bf16),
        compiler_params=LIMIT,
        cost_estimate=pl.CostEstimate(flops=1000000, bytes_accessed=1500000, transcendentals=0),
    )(values)


LINE_ROWS = 704
EXPERT_ROWS = 384
STEP = 256


def rows_of(a, b, count):
    return dot_outer(a[...], b[...]).reshape(SLOTS, count, -1)


def put(out_ref, first, parts):
    value = jnp.concatenate(parts, axis=1).astype(bf16)
    out_ref[:, first : first + value.shape[1]] = value


def expert_products_kernel(a_rows, b_due0, b_due1, b_due2, b_due3, a_hidden, b_rows, out_ref):
    put(out_ref, 0, [rows_of(a_rows, b, 48) for b in (b_due0, b_due1, b_due2, b_due3)])
    put(out_ref, 192, [rows_of(a_hidden, b_rows, 192)])


def shared_products_kernel(
    a_qkv, b_q, b_k, b_v, a_out, b_out, a_in, b_in0, b_in1, b_in2, b_in3, a_zero, b_zero, a_second, b_second,
    buffer_ref, out_ref, staged,
):
    block = pl.program_id(1)

    @pl.when(block == 0)
    def _():
        put(staged, 0, [rows_of(a_qkv, b, 24) for b in (b_q, b_k, b_v)] + [rows_of(a_out, b_out, 24)])
        put(staged, 96, [rows_of(a_in, b, 24) for b in (b_in0, b_in1, b_in2, b_in3)])
        zero = rows_of(a_zero, b_zero, 24)
        put(staged, 192, [zero, jnp.zeros_like(zero[:, :8])])
        second = dot_outer(a_second[...], b_second[...]).reshape(12, SLOTS, 8, -1)
        put(staged, 224, [second[j] for j in range(12)])

    out_ref[...] = staged[:, pl.ds(pl.multiple_of(block * 64, 64), 64), :]


def product_operands(pairs, counts):
    operands, specs, flops = [], [], 0
    for (a, b), count in zip(pairs, counts):
        operands.append(a)
        specs.append(pl.BlockSpec(a.shape, lambda n, *rest: (0, 0)))
        flops += 2 * a.size * b.shape[1]
        for j in range(count):
            operands.append(b)
            specs.append(
                pl.BlockSpec((b.shape[0], STEP), lambda n, *rest, j=j: (0, n + j * (WIDTH // STEP)))
            )
    return operands, specs, flops


def expert_products(expert_in, expert_out):
    operands, specs, flops = product_operands((expert_in, expert_out), (4, 1))
    return pl.pallas_call(
        expert_products_kernel,
        grid=(WIDTH // STEP,),
        in_specs=specs,
        out_specs=pl.BlockSpec((SLOTS, EXPERT_ROWS, STEP), lambda n: (0, 0, n)),
        out_shape=jax.ShapeDtypeStruct((SLOTS, LINE_ROWS, WIDTH), bf16),
        compiler_params=LIMIT,
        cost_estimate=pl.CostEstimate(flops=flops, bytes_accessed=15000000, transcendentals=0),
    )(*operands)


def shared_products(pairs, buffer):
    operands, specs, flops = product_operands(pairs, (3, 1, 4, 1, 1))
    return pl.pallas_call(
        shared_products_kernel,
        grid=(WIDTH // STEP, (LINE_ROWS - EXPERT_ROWS) // 64),
        in_specs=specs + [pl.BlockSpec(memory_space=pl.ANY)],
        out_specs=pl.BlockSpec((SLOTS, 64, STEP), lambda n, r: (0, EXPERT_ROWS // 64 + r, n)),
        out_shape=jax.ShapeDtypeStruct((SLOTS, LINE_ROWS, WIDTH), bf16),
        scratch_shapes=[pltpu.VMEM((SLOTS, LINE_ROWS - EXPERT_ROWS, STEP), bf16)],
        input_output_aliases={len(operands): 0},
        compiler_params=LIMIT,
        cost_estimate=pl.CostEstimate(flops=flops, bytes_accessed=15000000, transcendentals=0),
    )(*operands, buffer)


def expert_kernel(
    arrived_ref, w_in_ref, w_out_ref, produced_ref, rows_ref, grads_ref, hidden_ref, due_ref, forward_acc, back_acc
):
    step = pl.program_id(0)

    @pl.when(step == 0)
    def _():
        whole = arrived_ref[...].astype(f32)
        rows_ref[...] = whole[:, :40].reshape(320, WIDTH).astype(bf16)
        grads_ref[...] = whole[:, 40:].reshape(320, WIDTH).astype(bf16)
        forward_acc[...] = jnp.zeros_like(forward_acc)
        back_acc[...] = jnp.zeros_like(back_acc)

    u = dot(rows_ref[...], w_in_ref[...])
    grad_hidden = dot_back(grads_ref[...], w_out_ref[...])
    hidden, slope = gelu_pair(u)
    hidden = hidden.astype(bf16)
    due = (grad_hidden * slope).astype(bf16)
    hidden_ref[...] = hidden
    due_ref[...] = due
    forward_acc[...] += dot(hidden, w_out_ref[...])
    back_acc[...] += dot_back(due, w_in_ref[...])

    @pl.when(step == pl.num_programs(0) - 1)
    def _():
        parts = [a[...].reshape(EXPERTS, 40, WIDTH) for a in (forward_acc, back_acc)]
        produced_ref[...] = jnp.concatenate(parts, axis=1).astype(bf16)


def expert_block(arrived, w_in, w_out):
    def fixed(shape):
        return pl.BlockSpec(shape, lambda n: (0,) * len(shape))

    rows = jax.ShapeDtypeStruct((320, WIDTH), bf16)
    units = jax.ShapeDtypeStruct((320, FF), bf16)
    return pl.pallas_call(
        expert_kernel,
        grid=(FF // 512,),
        in_specs=[
            fixed((EXPERTS, 80, WIDTH)),
            pl.BlockSpec((WIDTH, 512), lambda n: (0, n)),
            pl.BlockSpec((512, WIDTH), lambda n: (n, 0)),
        ],
        out_specs=(
            fixed((EXPERTS, 80, WIDTH)),
            fixed((320, WIDTH)),
            fixed((320, WIDTH)),
            pl.BlockSpec((320, 512), lambda n: (0, n)),
            pl.BlockSpec((320, 512), lambda n: (0, n)),
        ),
        out_shape=(jax.ShapeDtypeStruct((EXPERTS, 80, WIDTH), bf16), rows, rows, units, units),
        scratch_shapes=[pltpu.VMEM((320, WIDTH), f32), pltpu.VMEM((320, WIDTH), f32)],
        compiler_params=LIMIT,
        cost_estimate=pl.CostEstimate(
            flops=8 * 320 * WIDTH * FF, bytes_accessed=15000000, transcendentals=320 * FF
        ),
    )(arrived, w_in, w_out)


UNITS = 512


def dense_forward_kernel(c_ref, w_in_ref, w_out_ref, u_ref, hidden_ref, out_ref):
    @pl.when(pl.program_id(0) == 0)
    def _():
        out_ref[...] = jnp.zeros_like(out_ref)

    u = dot(c_ref[...], w_in_ref[...])
    hidden = gelu(u).astype(bf16)
    u_ref[...] = u
    hidden_ref[...] = hidden
    out_ref[...] += dot(hidden, w_out_ref[...])


def dense_backward_kernel(grad_ref, u_ref, w_in_ref, w_out_ref, du_ref, out_ref):
    @pl.when(pl.program_id(0) == 0)
    def _():
        out_ref[...] = jnp.zeros_like(out_ref)

    slope = gelu_pair(u_ref[...])[1]
    du = (dot_back(grad_ref[...], w_out_ref[...]) * slope).astype(bf16)
    du_ref[...] = du
    out_ref[...] += dot_back(du, w_in_ref[...])


def dense_specs():
    return (
        pl.BlockSpec((1024, UNITS), lambda n: (0, 8 * WIDTH // UNITS + n)),
        pl.BlockSpec((UNITS, WIDTH), lambda n: (n % 2, 12 + n // 2)),
        pl.BlockSpec((ROWS, UNITS), lambda n: (0, n)),
    )


def dense_call(kernel, in_specs, out_specs, out_shape, operands):
    return pl.pallas_call(
        kernel,
        grid=(FF // UNITS,),
        in_specs=in_specs,
        out_specs=out_specs,
        out_shape=out_shape,
        compiler_params=LIMIT,
        cost_estimate=pl.CostEstimate(
            flops=2 * ROWS * FF * 1792, bytes_accessed=14000000, transcendentals=ROWS * FF
        ),
    )(*operands)


def dense_forward(c, shared):
    w_in, w_out, units = dense_specs()
    return dense_call(
        dense_forward_kernel,
        [pl.BlockSpec((ROWS, 1024), lambda n: (0, 0)), w_in, w_out],
        (units, units, pl.BlockSpec((ROWS, WIDTH), lambda n: (0, 0))),
        (
            jax.ShapeDtypeStruct((ROWS, FF), f32),
            jax.ShapeDtypeStruct((ROWS, FF), bf16),
            jax.ShapeDtypeStruct((ROWS, WIDTH), f32),
        ),
        (c, shared, shared),
    )


def dense_backward(grad, u, shared):
    w_in, w_out, units = dense_specs()
    return dense_call(
        dense_backward_kernel,
        [pl.BlockSpec((ROWS, WIDTH), lambda n: (0, 0)), units, w_in, w_out],
        (units, pl.BlockSpec((ROWS, 1024), lambda n: (0, 0))),
        (jax.ShapeDtypeStruct((ROWS, FF), bf16), jax.ShapeDtypeStruct((ROWS, 1024), f32)),
        (grad, u, shared, shared),
    )


def staging(dtype, count):
    return [pltpu.VMEM((GROUP, 2 * HEAD_DIM), dtype)] * count


def head_forward(blocks, bias, start):
    return pl.pallas_call(
        forward_kernel,
        out_shape=(
            jax.ShapeDtypeStruct((GROUP, 2 * HEAD_DIM), bf16),
            jax.ShapeDtypeStruct((GROUP, MICRO), f32),
        ),
        scratch_shapes=staging(bf16, 3),
        compiler_params=LIMIT,
        cost_estimate=pl.CostEstimate(
            flops=4 * MICRO * GROUP * GROUP * HEAD_DIM // 2,
            bytes_accessed=6 * GROUP * 256,
            transcendentals=MICRO * GROUP * GROUP // 2,
        ),
    )(blocks, bias, start)


def head_backward(blocks, grad_o, bias, start, lse):
    return pl.pallas_call(
        backward_kernel,
        out_shape=(
            jax.ShapeDtypeStruct((SLOTS, 3 * TOK, 2 * HEAD_DIM), bf16),
            jax.ShapeDtypeStruct((BLOCK, GROUP), f32),
        ),
        scratch_shapes=staging(bf16, 3)
        + staging(f32, 3)
        + [pltpu.VMEM((GROUP, HEAD_DIM), f32), pltpu.VMEM((GROUP, HEAD_DIM), f32)],
        compiler_params=LIMIT,
        cost_estimate=pl.CostEstimate(
            flops=10 * MICRO * GROUP * GROUP * HEAD_DIM // 2,
            bytes_accessed=12 * GROUP * 256,
            transcendentals=MICRO * GROUP * GROUP // 2,
        ),
    )(blocks, grad_o, bias, start, lse)


def tile_distance():
    row = lax.broadcasted_iota(jnp.int32, (BLOCK, GROUP), 0)
    column = lax.broadcasted_iota(jnp.int32, (BLOCK, GROUP), 1)
    return row - column + (GROUP - BLOCK)


def bucket_starts():
    return [0, 1, 2, 3, 4, 5, 6, 7] + [2**t for t in range(3, 11)]


def bias_tile(entries):
    distance = tile_distance()
    result = jnp.full((BLOCK, GROUP), NEGATIVE, f32)
    for b, first in enumerate(bucket_starts()):
        result = jnp.where(distance >= first, entries[b], result)
    return result


def table_sums(tile):
    distance = tile_distance()
    first = jnp.array(bucket_starts(), jnp.int32)[:, None, None]
    last = jnp.array(bucket_starts()[1:] + [GROUP], jnp.int32)[:, None, None]
    inside = (distance[None] >= first) & (distance[None] < last)
    return jnp.sum(jnp.where(inside, tile[None], 0.0), axis=(1, 2))


def exchange(blocks, axes):
    return lax.all_to_all(blocks, axes, split_axis=0, concat_axis=0, tiled=True)


def spread_matrix():
    out = lax.broadcasted_iota(jnp.int32, (WIDTH, 1024), 1)
    source = lax.broadcasted_iota(jnp.int32, (WIDTH, 1024), 0)
    return ((out % 8 < 6) & (source == out // 8 * 6 + out % 8)).astype(bf16)


def spread(values, places):
    return dot(values, places).astype(bf16)


def gather_back(values, places):
    return dot_back(values.astype(bf16), places)


HEAD_SHAPE = (SLOTS, 3 * TOK, 2 * HEAD_DIM)
ONE_SHAPE = (SLOTS, TOK, 2 * HEAD_DIM)


def attend_forward(x, scales, w_qkv, w_out, places, bias, start):
    normed, inv = normalize(x, scales)
    blocks = exchange(repack(pack_qkv_kernel, HEAD_SHAPE, dot(spread(normed, places), w_qkv)), LINE)
    o, lse = head_forward(blocks, bias, start)
    attended = repack(unpack_one_kernel, (ROWS, WIDTH), exchange(o.reshape(ONE_SHAPE), LINE))
    x = x + dot(spread(attended, places), w_out)
    return x, (normed, inv, blocks, lse, attended)


def attend_backward(grad, x, scales, w_qkv, w_out, places, bias, start, saved):
    normed, inv, blocks, lse, attended = saved
    branch = grad.astype(bf16)
    grad_attended = gather_back(dot_back(branch, w_out), places)
    grad_o = exchange(repack(pack_one_kernel, ONE_SHAPE, grad_attended), LINE)
    grad_heads, tile = head_backward(blocks, grad_o.reshape(GROUP, 2 * HEAD_DIM), bias, start, lse)
    heads = repack(unpack_qkv_kernel, (ROWS, 3 * WIDTH), exchange(grad_heads, LINE))
    grad_normed = gather_back(dot_back(heads, w_qkv), places)
    grad_x, grad_scales = normalize_back(grad_normed, x, inv, scales)
    return grad + grad_x, grad_scales, branch, heads, tile


def other_core(value):
    return lax.ppermute(value, "c", [(0, 1), (1, 0)])


def select_columns(core, line_first):
    out = lax.broadcasted_iota(jnp.int32, (WIDTH, WIDTH // 2), 1)
    source = lax.broadcasted_iota(jnp.int32, (WIDTH, WIDTH // 2), 0)
    outer, i = out // 6, out % 6
    z, line = (outer % 4, outer // 4) if line_first else (outer // SLOTS, outer % SLOTS)
    return (source == ((z * 2 + core) * SLOTS + line) * 6 + i).astype(bf16)


def pick(a, selector):
    return dot(a, selector).astype(bf16)


def on_device(
    hidden_in, lengths, routes, norm_gains, qkv_weights, out_weights, rel_table,
    ffn_in, ffn_out, router, expert_in, expert_out, cotangent,
):
    core = lax.axis_index("c")
    line_rank = lax.axis_index("y") * 4 + lax.axis_index("x")

    places = spread_matrix()
    ffn_in_units = ffn_in.reshape(6, 128, 3, 8).transpose(0, 2, 1, 3).reshape(6, FF)
    attention = [
        jnp.concatenate([qkv_weights[l, 0], qkv_weights[l, 1], qkv_weights[l, 2], out_weights[l]], axis=1)
        for l in range(2)
    ]
    pack = jnp.pad(jnp.concatenate(attention + [ffn_in_units], axis=1), ((0, 2), (0, 0)))
    pack = jnp.concatenate([pack, ffn_out[:8], ffn_out[8:16], ffn_out[16:]], axis=1)
    shared = lax.all_gather(pack, ALL, axis=0, tiled=True)
    w_expert_in = lax.all_gather(expert_in[0], LINE, axis=0, tiled=True)
    w_expert_out = lax.all_gather(expert_out[0], LINE, axis=0, tiled=True)
    qkv_zero, out_zero = shared[:, : 3 * WIDTH], shared[:, 3 * WIDTH : 4 * WIDTH]
    qkv_one, out_one = shared[:, 4 * WIDTH : 7 * WIDTH], shared[:, 7 * WIDTH : 8 * WIDTH]

    small = jnp.concatenate([norm_gains.reshape(24), router.reshape(48), rel_table])
    small = jnp.pad(small, (0, 128 - 75))[None, None, :]
    small = jnp.broadcast_to(small, (SLOTS, 8, 128))
    small = exchange(small, LINE).reshape(1, 128, 128)
    small = exchange(jnp.broadcast_to(small, (EXPERTS, 128, 128)), ROW)
    small = small.reshape(128, 8, 128)[:, 0]
    gains = small[:, :24].reshape(128, 4, 6).transpose(1, 0, 2).reshape(4, WIDTH).astype(f32)
    w_router = small[:, 24:72].reshape(WIDTH, EXPERTS)
    table = small[:, 72:75].reshape(2, HEADS, BUCKETS).astype(f32)
    head = jnp.minimum(line_rank, HEADS - 1)
    entries = lax.dynamic_index_in_dim(table, head, axis=1, keepdims=False)
    bias = [bias_tile(entries[layer]) for layer in range(2)]

    ends = jnp.cumsum(lengths[:, 0], axis=1)
    position = jnp.arange(GROUP, dtype=jnp.int32)[:, None, None]
    start = jnp.max(jnp.where(position >= ends[None], ends[None], 0), axis=2)

    x0 = hidden_in.reshape(ROWS, WIDTH).astype(f32)
    x1, saved_one = attend_forward(x0, gains[0], qkv_zero, out_zero, places, bias[0], start)
    c, inv_c = normalize(x1, gains[1])
    u, h, dense_out = dense_forward(spread(c, places), shared)
    x2 = x1 + dense_out
    x3, saved_three = attend_forward(x2, gains[2], qkv_one, out_one, places, bias[1], start)

    e, inv_e = normalize(x3, gains[3])
    logits = dot(e, w_router)
    choice = routes.reshape(ROWS, 2)
    marks = (choice[:, :, None] == jnp.arange(EXPERTS, dtype=jnp.int32)).astype(f32)
    chosen = jnp.sum(marks * logits[:, None, :], axis=-1)
    gates = jax.nn.softmax(chosen, axis=-1)
    pair_marks = marks.reshape(MICRO, TOK * 2, EXPERTS)
    earlier = jnp.cumsum(pair_marks, axis=1) - pair_marks
    slots = jnp.sum(earlier * pair_marks, axis=-1).astype(jnp.int32).reshape(ROWS, 2)
    micro = (jnp.arange(ROWS, dtype=jnp.int32) // TOK)[:, None]
    target = choice * 80 + micro * CAP + slots
    target_k = target.T
    row_id = jnp.arange(EXPERTS * 80, dtype=jnp.int32)
    place = [row_id[:, None] == target_k[k][None, :] for k in range(2)]
    place_back = [row_id[:, None] == target_k[k][None, :] + 40 for k in range(2)]
    scatter = jnp.concatenate([place[0] | place[1], place_back[0], place_back[1]], axis=1).astype(bf16)
    collect = jnp.concatenate([place_back[0] | place_back[1], place[0], place[1]], axis=1).astype(bf16)
    grad_four = cotangent.reshape(ROWS, WIDTH).astype(f32)
    picked_grads = [(gates[:, k : k + 1] * grad_four).astype(bf16) for k in range(2)]
    sent = dot(scatter, jnp.concatenate([e] + picked_grads, axis=0)).astype(bf16)
    arrived = exchange(sent.reshape(EXPERTS, 80, WIDTH), ROW)
    produced, expert_rows, grad_rows, he, due = expert_block(arrived, w_expert_in, w_expert_out)
    buffer = expert_products((expert_rows, due), (he, grad_rows))
    returned = exchange(produced, ROW).reshape(EXPERTS * 80, WIDTH)
    collected = dot_outer(collect, returned)
    picked = [collected[ROWS : 2 * ROWS], collected[2 * ROWS :]]
    hidden_out = x3 + gates[:, :1] * picked[0] + gates[:, 1:] * picked[1]

    dgates = jnp.stack([jnp.sum(grad_four * p, axis=-1) for p in picked], axis=1)
    dchosen = gates * (dgates - jnp.sum(gates * dgates, axis=-1, keepdims=True))
    dlogits = jnp.sum(marks * dchosen[:, :, None], axis=1)
    grad_router = dot_outer(e, dlogits.astype(bf16))
    grad_e = collected[:ROWS] + dot_back(dlogits.astype(bf16), w_router)
    grad_x, gain_four = normalize_back(grad_e, x3, inv_e, gains[3])
    grad_three = grad_four + grad_x + 0.0 * buffer[0, 0, 0].astype(f32)


    def share(a, b, line_first):
        mine = pick(a, select_columns(core, line_first))
        theirs = pick(a, select_columns(1 - core, line_first))
        got = other_core(jnp.concatenate([theirs, b], axis=1))
        return (
            jnp.concatenate([mine, got[:, : WIDTH // 2]], axis=0),
            jnp.concatenate([b, got[:, WIDTH // 2 :]], axis=0),
        )

    def chunks(a, b, count):
        return [
            dot_outer(a, b[:, j * WIDTH : (j + 1) * WIDTH]).astype(bf16).reshape(count, -1, WIDTH)
            for j in range(b.shape[1] // WIDTH)
        ]

    grad_two, gain_three, branch_three, heads_three, tile_three = attend_backward(
        grad_three, x2, gains[2], qkv_one, out_one, places, bias[1], start, saved_three
    )
    pair_qkv = share(saved_three[0], heads_three, True)
    pair_out = share(saved_three[4], branch_three, True)

    branch_two = grad_two.astype(bf16)
    du, grad_c = dense_backward(branch_two, u, shared)
    grad_c = gather_back(grad_c, places)
    grad_x, gain_two = normalize_back(grad_c, x1, inv_c, gains[1])
    grad_one = grad_two + grad_x
    pair_in = share(c, du, True)
    pair_zero = share(saved_one[4], grad_one.astype(bf16), True)
    halves = h.reshape(ROWS, 12, 2, BLOCK)
    mine = lax.dynamic_index_in_dim(halves, core, axis=2, keepdims=False).reshape(ROWS, FF // 2)
    theirs = lax.dynamic_index_in_dim(halves, 1 - core, axis=2, keepdims=False).reshape(ROWS, FF // 2)
    got = other_core(jnp.concatenate([theirs, branch_two], axis=1))
    mine = jnp.concatenate([mine, got[:, : FF // 2]], axis=0)
    pair_second = (mine, jnp.concatenate([branch_two, got[:, FF // 2 :]], axis=0))
    summed = shared_products((pair_qkv, pair_out, pair_in, pair_zero, pair_second), buffer)
    early_sum = lax.optimization_barrier(
        lax.psum_scatter(summed, LINE, scatter_dimension=0, tiled=False)
    )
    expert_sum, early_sum = early_sum[:EXPERT_ROWS], early_sum[EXPERT_ROWS:]

    grad_zero, gain_one, branch_one, heads_one, tile_one = attend_backward(
        grad_one, x0, gains[0], qkv_zero, out_zero, places, bias[0], start, saved_one
    )
    late = chunks(*share(saved_one[0], heads_one, False), 64)

    own_head = (jnp.arange(HEADS, dtype=jnp.int32) == line_rank).astype(f32)
    table_grad = jnp.stack([table_sums(tile_one), table_sums(tile_three)])
    table_grad = (own_head[None, :, None] * table_grad[:, None, :]).reshape(128, 3)
    gain_grad = jnp.stack([gain_one, gain_two, gain_three, gain_four])
    gain_grad = gain_grad.reshape(4, 128, 6).transpose(1, 0, 2).reshape(128, 24)
    tiny = jnp.concatenate([gain_grad, grad_router.reshape(128, 48), table_grad], axis=1)
    tiny = jnp.pad(tiny, ((0, 0), (0, 128 - 75))).reshape(4, 2, SLOTS, 128)
    tiny_mine = lax.dynamic_index_in_dim(tiny, core, axis=1, keepdims=False)
    tiny_theirs = lax.dynamic_index_in_dim(tiny, 1 - core, axis=1, keepdims=False)
    tiny_sum = tiny_mine + other_core(tiny_theirs)
    tiny_sum = jnp.pad(tiny_sum.reshape(64, 1, 128), ((0, 0), (0, 5), (0, WIDTH - 128)))
    late_blocks = exchange(jnp.concatenate(late + [tiny_sum.astype(bf16)], axis=1), ("z", "y", "x"))
    late_sum = jnp.sum(late_blocks.astype(f32), axis=0)
    tiny = late_sum[18, :75]

    early_rows = early_sum[:216].reshape(9, 4, 6, WIDTH).transpose(1, 0, 2, 3).reshape(4, 54, WIDTH)
    ffn_out_rows = early_sum[224:320].reshape(3, 4, 8, WIDTH).transpose(1, 0, 2, 3).reshape(4, 24, WIDTH)
    last = jnp.concatenate([ffn_out_rows, early_rows], axis=1)
    last = exchange(jnp.pad(last, ((0, 0), (0, 2), (0, 0))), ("z",))
    last = jnp.sum(last.astype(f32), axis=0)
    six = last[24:78].reshape(9, 6, WIDTH)
    ffn_in_part = six[4:8].transpose(1, 0, 2).reshape(6, 3, 128, 8).transpose(0, 2, 1, 3)
    out_shape = hidden_in.shape
    return (
        hidden_out.reshape(out_shape),
        grad_zero.reshape(out_shape),
        tiny[:24].reshape(4, 6),
        jnp.stack([late_sum[:18].reshape(3, 6, WIDTH), six[0:3]]),
        jnp.stack([six[8], six[3]]),
        tiny[72:75],
        ffn_in_part.reshape(6, FF),
        last[:24],
        tiny[24:72].reshape(6, EXPERTS),
        expert_sum[:192].astype(f32).reshape(4, 48, WIDTH).transpose(1, 0, 2).reshape(1, 48, FF),
        expert_sum[192:].astype(f32).reshape(1, 192, WIDTH),
    )


def solution(mesh):
    fine = Mesh(mesh.devices.reshape(4, 2, 4, 4), ALL)
    return jax.shard_map(
        on_device,
        mesh=fine,
        in_specs=(
            P(None, ALL, None),
            P(None, ROW, None),
            P(None, ALL, None),
            P(None, ALL),
            P(None, None, ALL, None),
            P(None, ALL, None),
            P(ALL),
            P(ALL, None),
            P(ALL, None),
            P(ALL, None),
            P(ROW, LINE, None),
            P(ROW, LINE, None),
            P(None, ALL, None),
        ),
        out_specs=(
            P(None, ALL, None),
            P(None, ALL, None),
            P(None, ALL),
            P(None, None, ALL, None),
            P(None, ALL, None),
            P(ALL),
            P(ALL, None),
            P(ALL, None),
            P(ALL, None),
            P(ROW, LINE, None),
            P(ROW, LINE, None),
        ),
        check_vma=False,
    )
```
